32 devices in a mesh: grp: 2 (over y), seq: 8 (over z, x), outer: 2 (over core).
Axes of the slice: x: 2, y: 2, z: 4, core: 2. Of those that a mesh axis runs over, the one named last changes fastest.
Arguments:
- keys: bfloat16 [4096, 512], P(('grp', 'seq', 'outer')), parts along dimension 0, may hold values from -6 to 6
- values: bfloat16 [4096, 512], P(('grp', 'seq', 'outer')), parts along dimension 0, may hold values from -6 to 6
- queries: bfloat16 [4096, 512], P(('grp', 'seq', 'outer')), parts along dimension 0, may hold values from -6 to 6
- learn_rate: float32 [4096], P(('grp', 'seq', 'outer')), parts along dimension 0, may hold values from 0.0006629126 to 0.006629126
- w_gate: bfloat16 [1024, 512], P('grp'), parts along dimension 0, may hold values from -0.25 to 0.25
- w_up: bfloat16 [1024, 512], P('grp'), parts along dimension 0, may hold values from -0.25 to 0.25
- w_out: bfloat16 [1024, 512], P('grp'), parts along dimension 0, may hold values from -0.25 to 0.25
Outputs:
- output: bfloat16 [4096, 512], P(('grp', 'seq', 'outer')), parts along dimension 0
The draws below stay inside these ranges and needn't reach their ends.
There are 2 independent parts, one for each index of `grp`. The reference program is written for one: setup_inputs(seed, part) draws one part's arguments, and reference() takes and returns one part's arrays. A program takes and returns all parts, laid end to end along the dimension named above; each array names one. Nothing has to cross between parts.
All inputs are finite; a program needn't handle non-finite values.
Results may differ from the reference program's by a relative error of at most 0.0098.
Values may be sent and summed in bfloat16 or wider, within the bound.
A program may use at most 64 MiB of HBM per device.

```python
import math
import jax
import jax.numpy as jnp
from jax import lax

D = 512
HID = 512
TOKENS = 2048


def raised(values, stream_key, source, target, shards_of, factor):
    owner, partner = [(jnp.arange(values.shape[axis_at]) // (values.shape[axis_at] // shards_of)).reshape([-1 if axis == axis_at else 1 for axis in range(values.ndim)]) for axis_at in (source, target)]
    chosen = jax.random.permutation(stream_key, shards_of)[partner]
    strong = (owner == chosen) | (owner == (partner + shards_of // 2) % shards_of)
    return jnp.where(strong, factor * values, values)


def block_scale(stream_key, extent, split, low, high):
    def one(position, shards_of):
        steps = jax.random.uniform(jax.random.fold_in(jax.random.fold_in(stream_key, 6), position), (shards_of,), jnp.float32, low / len(split), high / len(split))
        return jnp.repeat(jnp.exp(steps), extent[position] // shards_of).reshape((-1,) + (1,) * (len(extent) - position - 1))

    loudness = one(*split[0])
    for cut in split[1:]:
        loudness = loudness * one(*cut)
    return loudness


def normal_values(key, shape, deviation, limit, pieces=(), kind=jnp.bfloat16):
    factor_of = block_scale(key, shape, pieces, -0.22, 0.18) if pieces else 1.0
    entries = jax.random.normal(key, shape, jnp.float32) * deviation * factor_of
    return jnp.minimum(jnp.maximum(entries, -limit), limit).astype(kind)


def noise_with(stream_key, dims, scale, limit, cuts, heavy, dtype=jnp.bfloat16):
    entries = scale * jax.random.normal(stream_key, dims, jnp.float32)
    if cuts:
        entries = entries * block_scale(stream_key, dims, cuts, -0.22, 0.18)
    return jnp.clip(raised(entries, jax.random.fold_in(stream_key, 3), *heavy), -limit, limit).astype(dtype)


def setup_inputs(seed: int = 0, part: int = 0) -> dict:
    key_list = jax.random.split(jax.random.key(seed), 8)
    part_splits = jax.random.split(jax.random.fold_in(key_list[7], part), 8)
    keys = noise_with(part_splits[0], (TOKENS, D), 1.0, 6.0, ((0, 16),), (0, 1, 16, 2.0))
    values = noise_with(part_splits[1], (TOKENS, D), 1.0, 6.0, ((0, 16),), (0, 1, 16, 2.0))
    queries = normal_values(part_splits[2], (TOKENS, D), 1.0, 6.0, ((0, 16),))
    learn_rate = jnp.clip(jnp.exp(math.log(0.006629126) - 2.3025851 * jax.random.uniform(part_splits[3], (TOKENS,), jnp.float32) ** block_scale(part_splits[3], (TOKENS,), ((0, 16),), -0.2, 0.2)), 0.0006629126, 0.006629126)
    w_gate = normal_values(part_splits[4], (D, HID), D ** -0.5, 0.25)
    w_up = normal_values(part_splits[5], (D, HID), D ** -0.5, 0.25)
    w_out = normal_values(part_splits[6], (HID, D), HID ** -0.5, 0.25)
    return dict(keys=keys, values=values, queries=queries, learn_rate=learn_rate, w_gate=w_gate, w_up=w_up, w_out=w_out)


epsilon = 1e-06

def silu_grad(inputs):
    sigma = jax.nn.sigmoid(inputs)
    return sigma * (1.0 + inputs * (1.0 - sigma))

def renorm(weight, grads):
    old = weight.astype(jnp.float32)
    update = old + grads
    factor = jnp.sqrt(lax.optimization_barrier(jnp.mean(old * old, axis=1, keepdims=True)) + epsilon) / jnp.sqrt(lax.optimization_barrier(jnp.mean(update * update, axis=1, keepdims=True)) + epsilon)
    return (update * factor).astype(jnp.bfloat16)

def reference(keys, values, queries, learn_rate, w_gate, w_up, w_out):
    total = keys.shape[0]
    block = min(4096, total)
    number = total // block
    width = keys.shape[1]
    hidden = w_gate.shape[1]
    key_blocks = keys.reshape(number, block, width)
    value_blocks = values.reshape(number, block, width)
    rate_blocks = learn_rate.reshape(number, block)

    def accumulate(totals, blocks):
        key_block, value_block, rate_block = blocks
        gate_pre = jnp.dot(key_block, w_gate, preferred_element_type=jnp.float32)
        up_pre = jnp.dot(key_block, w_up, preferred_element_type=jnp.float32)
        activation = (jax.nn.silu(gate_pre) * up_pre).astype(jnp.bfloat16)
        scaled = (rate_block[:, None] * value_block.astype(jnp.float32)).astype(jnp.bfloat16)
        back_grad = jnp.dot(scaled, w_out.T, preferred_element_type=jnp.float32)
        d_gate = (back_grad * up_pre * silu_grad(gate_pre)).astype(jnp.bfloat16)
        d_up = (back_grad * jax.nn.silu(gate_pre)).astype(jnp.bfloat16)
        grad_gate = totals[0] + jnp.dot(key_block.T, d_gate, preferred_element_type=jnp.float32)
        grad_up = totals[1] + jnp.dot(key_block.T, d_up, preferred_element_type=jnp.float32)
        grad_out = totals[2] + jnp.dot(activation.T, scaled, preferred_element_type=jnp.float32)
        return ((grad_gate, grad_up, grad_out), None)
    start_sums = (jnp.zeros((width, hidden), jnp.float32), jnp.zeros((width, hidden), jnp.float32), jnp.zeros((hidden, width), jnp.float32))
    sums, unused = lax.scan(accumulate, start_sums, (key_blocks, value_blocks, rate_blocks))
    new_gate = renorm(w_gate, sums[0])
    new_up = renorm(w_up, sums[1])
    new_out = renorm(w_out, sums[2])

    def apply_block(query_block):
        q_gate = jnp.dot(query_block, new_gate, preferred_element_type=jnp.float32)
        q_up = jnp.dot(query_block, new_up, preferred_element_type=jnp.float32)
        q_act = (jax.nn.silu(q_gate) * q_up).astype(jnp.bfloat16)
        return jnp.dot(q_act, new_out, preferred_element_type=jnp.float32).astype(jnp.bfloat16)
    result = lax.map(apply_block, queries.reshape(number, block, width))
    return result.reshape(total, width)
```

```python
import functools

import jax
import jax.numpy as jnp
from jax import lax
from jax.experimental import pallas as pl
from jax.experimental.pallas import tpu as pltpu
from jax.sharding import PartitionSpec as P

epsilon = 1e-06
MESH = pl.DeviceIdType.MESH
F32 = jnp.float32
BF16 = jnp.bfloat16
NT = (((1,), (1,)), ((), ()))
TN = (((0,), (0,)), ((), ()))


def silu_grad(inputs):
    sigma = jax.nn.sigmoid(inputs)
    return sigma * (1.0 + inputs * (1.0 - sigma))


def kernel(
    planes,
    lr_ref,
    k_ref,
    v_ref,
    q_ref,
    wg_ref,
    wu_ref,
    wo_ref,
    o_ref,
    kbuf,
    sbuf,
    qbuf,
    wcat,
    wback,
    old,
    acc_in,
    acc_out,
    gsend,
    grecv,
    stat,
    fact,
    wbuf,
    wq,
    wo,
    psend,
    precv,
    tok_send,
    tok_recv,
    q_send,
    q_recv,
    g_send,
    g_recv,
    st_send,
    st_recv,
    f_send,
    f_recv,
    w_send,
    w_recv,
    c_send,
    c_recv,
    p_send,
    p_recv,
):
    tokens, width = k_ref.shape
    hidden = wg_ref.shape[1]
    hb = hidden // 4
    db = width // planes
    rb = hb // planes
    spread = width // db
    seq = lax.axis_index("seq")
    core = lax.axis_index("outer")
    plane, side = seq // 2, seq % 2
    quarter = side * 2 + core
    cols = pl.ds(pl.multiple_of(quarter * hb, hb), hb)

    mate = {"outer": 1 - core}
    across = {"seq": plane * 2 + 1 - side}
    diagonal = {"seq": plane * 2 + 1 - side, "outer": 1 - core}

    def plane_at(distance):
        return (plane + distance) % planes

    def same_spot(distance):
        return {"seq": plane_at(distance) * 2 + side}

    barrier = pltpu.get_barrier_semaphore()
    peers = [mate, across, diagonal] + [same_spot(d) for d in range(1, planes)]
    for peer in peers:
        pl.semaphore_signal(barrier, inc=1, device_id=peer, device_id_type=MESH)

    def rows(slot):
        return pl.ds(slot * tokens, tokens)

    lr_cols = jnp.transpose(jnp.broadcast_to(lr_ref[...], (tokens, tokens)))
    rate = lr_cols[:, 0:1]
    sbuf[rows(0), :] = (rate * v_ref[...].astype(F32)).astype(BF16)
    kbuf[rows(0), :] = k_ref[...]
    pl.semaphore_wait(barrier, len(peers))

    def send(src, dst, send_sem, recv_sem, peer):
        copy = pltpu.make_async_remote_copy(
            src_ref=src,
            dst_ref=dst,
            send_sem=send_sem,
            recv_sem=recv_sem,
            device_id=peer,
            device_id_type=MESH,
        )
        copy.start()
        return copy

    def token_copy(buf, kind, src_slot, dst_slot, peer):
        return send(
            buf.at[rows(src_slot)],
            buf.at[rows(dst_slot)],
            tok_send.at[kind, dst_slot - 1],
            tok_recv.at[kind, dst_slot - 1],
            peer,
        )

    k_across = token_copy(kbuf, 0, 0, 2, across)
    s_across = token_copy(sbuf, 1, 0, 2, across)
    k_mate = token_copy(kbuf, 0, 0, 1, mate)
    s_mate = token_copy(sbuf, 1, 0, 1, mate)

    wcat[:, 0:hb] = wg_ref[:, cols]
    wcat[:, hb : 2 * hb] = wu_ref[:, cols]
    wback[...] = wo_ref[cols, :]

    my_cols = pl.ds(pl.multiple_of(plane * db, db), db)
    old_sums = []
    for i, ref in enumerate((wg_ref, wu_ref)):
        old[i * hb : (i + 1) * hb, :] = jnp.transpose(ref[my_cols, cols].astype(F32))
        whole = ref[my_cols, :].astype(F32)
        squares = whole * whole
        folded = squares[:, 0:hb]
        for j in range(1, 4):
            folded = folded + squares[:, j * hb : (j + 1) * hb]
        old_sums.append(jnp.sum(jnp.transpose(folded), axis=0, keepdims=True))
    old_out = wo_ref[pl.ds(pl.multiple_of(quarter * hb + plane * rb, rb), rb), :].astype(F32)

    def pre(span):
        both = jnp.dot(kbuf[span, :], wcat[...], preferred_element_type=F32)
        return both[:, 0:hb], both[:, hb : 2 * hb]

    def grads(span, gate_pre, up_pre):
        back = lax.dot_general(sbuf[span, :], wback[...], NT, preferred_element_type=F32)
        sigma = jax.nn.sigmoid(gate_pre)
        swish = gate_pre * sigma
        act = (swish * up_pre).astype(BF16)
        d_gate = (back * up_pre * (sigma * (1.0 + gate_pre * (1.0 - sigma)))).astype(BF16)
        d_up = (back * swish).astype(BF16)
        both = jnp.concatenate([d_gate, d_up], axis=1)
        g_in = lax.dot_general(both, kbuf[span, :], TN, preferred_element_type=F32)
        g_out = lax.dot_general(act, sbuf[span, :], TN, preferred_element_type=F32)
        return g_in, g_out

    k_mate.wait_recv()
    s_mate.wait_recv()
    first = slice(0, 2 * tokens)
    gate_pre, up_pre = pre(first)
    g_in, g_out = grads(first, gate_pre, up_pre)
    acc_in[...] = g_in
    acc_out[...] = g_out

    second = slice(2 * tokens, 4 * tokens)
    k_across.wait_recv()
    k_forward = token_copy(kbuf, 0, 2, 3, mate)
    k_forward.wait_recv()
    gate_pre, up_pre = pre(second)
    s_across.wait_recv()
    s_forward = token_copy(sbuf, 1, 2, 3, mate)
    q_copy = send(q_ref, qbuf.at[rows(1)], q_send, q_recv, across)
    s_forward.wait_recv()
    g_in, g_out = grads(second, gate_pre, up_pre)
    acc_in[...] += g_in
    acc_out[...] += g_out

    def part(p):
        top = acc_in[:, pl.ds(pl.multiple_of(p * db, db), db)]
        low = acc_out[pl.ds(pl.multiple_of(p * rb, rb), rb), :]
        return top, low

    g_copies = {}
    for d in (2, 1, 3) if planes == 4 else range(1, planes):
        top, low = part(plane_at(d))
        gsend[d - 1, 0 : 2 * hb, :] = top.astype(BF16)
        for j in range(spread):
            gsend[d - 1, 2 * hb + j * rb : 2 * hb + (j + 1) * rb, :] = low[
                :, j * db : (j + 1) * db
            ].astype(BF16)
        slot = planes - 1 - d
        g_copies[d] = send(
            gsend.at[d - 1], grecv.at[slot], g_send.at[d - 1], g_recv.at[slot], same_spot(d)
        )
    qbuf[rows(0), :] = q_ref[...]
    top, low = part(plane)
    sum_top = old[...] + top
    sum_low = [
        old_out[:, j * db : (j + 1) * db] + low[:, j * db : (j + 1) * db] for j in range(spread)
    ]
    for slot in range(planes - 1):
        g_copies[planes - 1 - slot].wait_recv()
        sum_top = sum_top + grecv[slot, 0 : 2 * hb, :].astype(F32)
        for j in range(spread):
            sum_low[j] = sum_low[j] + grecv[
                slot, 2 * hb + j * rb : 2 * hb + (j + 1) * rb, :
            ].astype(F32)

    squares = sum_top * sum_top
    mine = [
        jnp.sum(squares[i * hb : (i + 1) * hb, :], axis=0, keepdims=True) for i in range(2)
    ]
    stat[0] = jnp.concatenate([jnp.broadcast_to(one, (4, db)) for one in mine], axis=0)
    st_copies = [
        send(stat.at[0], stat.at[i + 1], st_send.at[i], st_recv.at[i], peer)
        for i, peer in enumerate((mate, across, diagonal))
    ]

    new_sum = sum(jnp.sum(one * one, axis=1, keepdims=True) for one in sum_low)
    old_sum = jnp.sum(old_out * old_out, axis=1, keepdims=True)
    factor = jnp.sqrt(old_sum / width + epsilon) / jnp.sqrt(new_sum / width + epsilon)
    wbuf[0, plane, 0 : 2 * hb, :] = sum_top.astype(BF16)
    for j in range(spread):
        wbuf[0, plane, 2 * hb + j * rb : 2 * hb + (j + 1) * rb, :] = (
            sum_low[j] * factor
        ).astype(BF16)

    w_copies = {}
    for d in (2, 1, 3) if planes == 4 else range(1, planes):
        slot = planes - 1 - d
        w_copies[d] = send(
            wbuf.at[0, plane], wbuf.at[0, plane], w_send.at[d - 1], w_recv.at[slot], same_spot(d)
        )

    def to_mate(index, p):
        return send(wbuf.at[0, p], wbuf.at[1, p], c_send.at[index], c_recv.at[index], mate)

    c_copies = [to_mate(0, plane)]

    for copy in st_copies:
        copy.wait_recv()
    total = stat[0] + stat[1] + stat[2] + stat[3]
    olds = jnp.concatenate([jnp.broadcast_to(one, (4, db)) for one in old_sums], axis=0)
    fact[plane] = jnp.sqrt(olds / hidden + epsilon) / jnp.sqrt(total / hidden + epsilon)
    f_copies = {}
    for d in range(1, planes):
        slot = planes - 1 - d
        f_copies[d] = send(
            fact.at[plane], fact.at[plane], f_send.at[d - 1], f_recv.at[slot], same_spot(d)
        )

    def arrived(buf, recv_sem, peer, send_sem):
        pltpu.make_async_remote_copy(
            src_ref=buf,
            dst_ref=buf,
            send_sem=send_sem,
            recv_sem=recv_sem,
            device_id=peer,
            device_id_type=MESH,
        ).wait_recv()

    def place(which, p):
        to = pl.ds(pl.multiple_of(p * db, db), db)
        for i in range(2):
            rows_of = slice(i * hb, (i + 1) * hb)
            scaled = wbuf[which, p, rows_of, :].astype(F32) * fact[p, 4 * i : 4 * i + 1, :]
            wq[which * 2 * hb + i * hb : which * 2 * hb + (i + 1) * hb, to] = scaled.astype(BF16)
        for j in range(spread):
            wo[pl.ds(pl.multiple_of(which * hb + p * rb, rb), rb), j * db : (j + 1) * db] = wbuf[
                which, p, 2 * hb + j * rb : 2 * hb + (j + 1) * rb, :
            ]

    place(0, plane)
    arrived(wbuf.at[1, plane], c_recv.at[0], mate, c_send.at[0])
    place(1, plane)
    order = (1, 3, 2) if planes == 4 else tuple(range(1, planes))
    for d in order:
        p = plane_at(d)
        arrived(wbuf.at[0, p], w_recv.at[d - 1], same_spot(d), w_send.at[d - 1])
        c_copies.append(to_mate(d, p))
        arrived(fact.at[p], f_recv.at[d - 1], same_spot(d), f_send.at[d - 1])
        place(0, p)
    q_copy.wait_recv()
    for d in order:
        p = plane_at(d)
        arrived(wbuf.at[1, p], c_recv.at[d], mate, c_send.at[d])
        place(1, p)

    def apply(span):
        pres = lax.dot_general(qbuf[span, :], wq[...], NT, preferred_element_type=F32)
        acts = []
        for which in range(2):
            gate = pres[:, which * 2 * hb : which * 2 * hb + hb]
            up = pres[:, which * 2 * hb + hb : (which + 1) * 2 * hb]
            acts.append((gate * jax.nn.sigmoid(gate) * up).astype(BF16))
        return jnp.dot(jnp.concatenate(acts, axis=1), wo[...], preferred_element_type=F32)

    psend[...] = apply(slice(tokens, 2 * tokens)).astype(BF16)
    p_copy = send(psend, precv, p_send, p_recv, across)
    own = apply(slice(0, tokens))
    p_copy.wait_recv()
    o_ref[...] = (own + precv[...].astype(F32)).astype(BF16)

    outgoing = [k_across, s_across, k_mate, s_mate, k_forward, s_forward, q_copy, p_copy]
    outgoing += list(g_copies.values()) + list(w_copies.values()) + list(f_copies.values())
    outgoing += st_copies + c_copies
    for copy in outgoing:
        copy.wait_send()


def fused(keys, values, queries, learn_rate, w_gate, w_up, w_out):
    tokens, width = keys.shape
    hidden = w_gate.shape[1]
    planes = lax.axis_size("seq") // 2
    hb, db = hidden // 4, width // planes
    part_rows = 3 * hb
    vmem = pltpu.VMEM
    dma = pltpu.SemaphoreType.DMA
    scratch = [
        vmem((4 * tokens, width), BF16),
        vmem((4 * tokens, width), BF16),
        vmem((2 * tokens, width), BF16),
        vmem((width, 2 * hb), BF16),
        vmem((hb, width), BF16),
        vmem((2 * hb, db), F32),
        vmem((2 * hb, width), F32),
        vmem((hb, width), F32),
        vmem((planes - 1, part_rows, db), BF16),
        vmem((planes - 1, part_rows, db), BF16),
        vmem((4, 8, db), F32),
        vmem((planes, 8, db), F32),
        vmem((2, planes, part_rows, db), BF16),
        vmem((4 * hb, width), BF16),
        vmem((2 * hb, width), BF16),
        vmem((tokens, width), BF16),
        vmem((tokens, width), BF16),
        dma((2, 3)),
        dma((2, 3)),
        dma,
        dma,
        dma((planes - 1,)),
        dma((planes - 1,)),
        dma((3,)),
        dma((3,)),
        dma((planes - 1,)),
        dma((planes - 1,)),
        dma((planes - 1,)),
        dma((planes - 1,)),
        dma((planes,)),
        dma((planes,)),
        dma,
        dma,
    ]
    return pl.pallas_call(
        functools.partial(kernel, planes),
        out_shape=jax.ShapeDtypeStruct((tokens, width), BF16),
        in_specs=[pl.BlockSpec(memory_space=pltpu.VMEM)] * 7,
        out_specs=pl.BlockSpec(memory_space=pltpu.VMEM),
        scratch_shapes=scratch,
        compiler_params=pltpu.CompilerParams(
            collective_id=0, has_side_effects=True, vmem_limit_bytes=40 * 2**20
        ),
        cost_estimate=pl.CostEstimate(
            flops=2 * tokens * width * hidden * 9, bytes_accessed=2 * 2**20, transcendentals=0
        ),
    )(learn_rate.reshape(1, tokens), keys, values, queries, w_gate, w_up, w_out)


def renorm(weight, grads):
    old = weight.astype(F32)
    update = old + grads
    factor = jnp.sqrt(jnp.mean(old * old, axis=1, keepdims=True) + epsilon) / jnp.sqrt(
        jnp.mean(update * update, axis=1, keepdims=True) + epsilon
    )
    return (update * factor).astype(BF16)


def plain(keys, values, queries, learn_rate, w_gate, w_up, w_out):
    hidden = w_gate.shape[1]
    axes = ("seq", "outer")
    shards = lax.axis_size(axes)
    rows_in, rows_out = w_gate.shape[0] // shards, w_out.shape[0] // shards
    position = lax.axis_index(axes)
    scaled = (learn_rate[:, None] * values.astype(F32)).astype(BF16)
    gate_pre = jnp.dot(keys, w_gate, preferred_element_type=F32)
    up_pre = jnp.dot(keys, w_up, preferred_element_type=F32)
    back = lax.dot_general(scaled, w_out, NT, preferred_element_type=F32)
    activation = (jax.nn.silu(gate_pre) * up_pre).astype(BF16)
    d_gate = (back * up_pre * silu_grad(gate_pre)).astype(BF16)
    d_up = (back * jax.nn.silu(gate_pre)).astype(BF16)
    both = jnp.concatenate([d_gate, d_up], axis=1)
    full_in = lax.dot_general(keys, both, TN, preferred_element_type=F32)
    full_out = lax.dot_general(activation, scaled, TN, preferred_element_type=F32)
    grad_in = lax.psum_scatter(full_in, axes, scatter_dimension=0, tiled=True)
    grad_out = lax.psum_scatter(full_out, axes, scatter_dimension=0, tiled=True)
    own_gate = lax.dynamic_slice_in_dim(w_gate, position * rows_in, rows_in, 0)
    own_up = lax.dynamic_slice_in_dim(w_up, position * rows_in, rows_in, 0)
    own_out = lax.dynamic_slice_in_dim(w_out, position * rows_out, rows_out, 0)
    news = (
        renorm(own_gate, grad_in[:, :hidden]),
        renorm(own_up, grad_in[:, hidden:]),
        renorm(own_out, grad_out),
    )
    gate, up, out = [lax.all_gather(new, axes, axis=0, tiled=True) for new in news]
    q_gate = jnp.dot(queries, gate, preferred_element_type=F32)
    q_up = jnp.dot(queries, up, preferred_element_type=F32)
    q_act = (jax.nn.silu(q_gate) * q_up).astype(BF16)
    return jnp.dot(q_act, out, preferred_element_type=F32).astype(BF16)


def local(keys, values, queries, learn_rate, w_gate, w_up, w_out):
    width, hidden = w_gate.shape
    tokens = keys.shape[0]
    seq, cores = lax.axis_size("seq"), lax.axis_size("outer")
    planes = seq // 2
    fits = (
        cores == 2
        and seq % 2 == 0
        and planes > 1
        and width % (128 * planes) == 0
        and hidden % (4 * 32 * planes) == 0
        and hidden // 4 == 128
        and tokens == 128
    )
    chosen = fused if fits else plain
    return chosen(keys, values, queries, learn_rate, w_gate, w_up, w_out)


def solution(mesh):
    placed = (
        P(("grp", "seq", "outer"), None),
        P(("grp", "seq", "outer"), None),
        P(("grp", "seq", "outer"), None),
        P(("grp", "seq", "outer")),
        P("grp", None),
        P("grp", None),
        P("grp", None),
    )
    return jax.shard_map(
        local,
        mesh=mesh,
        in_specs=placed,
        out_specs=P(("grp", "seq", "outer"), None),
        check_vma=False,
    )
```

```python
import functools

import jax
import jax.numpy as jnp
from jax import lax
from jax.experimental import pallas as pl
from jax.experimental.pallas import tpu as pltpu
from jax.sharding import PartitionSpec as P

epsilon = 1e-06
MESH = pl.DeviceIdType.MESH
F32 = jnp.float32
BF16 = jnp.bfloat16
NT = (((1,), (1,)), ((), ()))
TN = (((0,), (0,)), ((), ()))


def silu_grad(inputs):
    sigma = jax.nn.sigmoid(inputs)
    return sigma * (1.0 + inputs * (1.0 - sigma))


def kernel(
    planes,
    lr_ref,
    k_ref,
    v_ref,
    q_ref,
    wg_ref,
    wu_ref,
    wo_ref,
    o_ref,
    kbuf,
    sbuf,
    qbuf,
    wcat,
    wback,
    vbuf,
    lrbuf,
    wrows,
    old,
    acc_in,
    acc_out,
    gsend,
    grecv,
    stat,
    fact,
    wbuf,
    wq,
    wo,
    psend,
    precv,
    tok_send,
    tok_recv,
    q_send,
    q_recv,
    g_send,
    g_recv,
    st_send,
    st_recv,
    f_send,
    f_recv,
    w_send,
    w_recv,
    c_send,
    c_recv,
    p_send,
    p_recv,
    load,
):
    tokens, width = k_ref.shape
    hidden = wg_ref.shape[1]
    hb = hidden // 4
    db = width // planes
    rb = hb // planes
    spread = width // db
    seq = lax.axis_index("seq")
    core = lax.axis_index("outer")
    plane, side = seq // 2, seq % 2
    quarter = side * 2 + core
    cols = pl.ds(pl.multiple_of(quarter * hb, hb), hb)

    mate = {"outer": 1 - core}
    across = {"seq": plane * 2 + 1 - side}
    diagonal = {"seq": plane * 2 + 1 - side, "outer": 1 - core}

    def plane_at(distance):
        return (plane + distance) % planes

    def same_spot(distance):
        return {"seq": plane_at(distance) * 2 + side}

    def rows(slot):
        return pl.ds(slot * tokens, tokens)

    my_cols = pl.ds(pl.multiple_of(plane * db, db), db)
    moves = (
        (lr_ref, lrbuf),
        (v_ref, vbuf),
        (k_ref, kbuf.at[rows(0)]),
        (wg_ref.at[:, cols], wcat.at[:, 0:hb]),
        (wu_ref.at[:, cols], wcat.at[:, hb : 2 * hb]),
        (wo_ref.at[cols], wback),
        (wg_ref.at[my_cols], wrows.at[0]),
        (wu_ref.at[my_cols], wrows.at[1]),
        (q_ref, qbuf.at[rows(0)]),
    )
    loads = [pltpu.make_async_copy(a, b, load.at[i]) for i, (a, b) in enumerate(moves)]
    for copy in loads:
        copy.start()

    barrier = pltpu.get_barrier_semaphore()
    peers = [mate, across, diagonal] + [same_spot(d) for d in range(1, planes)]
    for peer in peers:
        pl.semaphore_signal(barrier, inc=1, device_id=peer, device_id_type=MESH)

    loads[0].wait()
    loads[1].wait()
    lr_cols = jnp.transpose(jnp.broadcast_to(lrbuf[...], (tokens, tokens)))
    rate = lr_cols[:, 0:1]
    sbuf[rows(0), :] = (rate * vbuf[...].astype(F32)).astype(BF16)
    pl.semaphore_wait(barrier, len(peers))

    def send(src, dst, send_sem, recv_sem, peer):
        copy = pltpu.make_async_remote_copy(
            src_ref=src,
            dst_ref=dst,
            send_sem=send_sem,
            recv_sem=recv_sem,
            device_id=peer,
            device_id_type=MESH,
        )
        copy.start()
        return copy

    def token_copy(src, buf, kind, dst_slot, peer):
        return send(
            src,
            buf.at[rows(dst_slot)],
            tok_send.at[kind, dst_slot - 1],
            tok_recv.at[kind, dst_slot - 1],
            peer,
        )

    k_across = token_copy(k_ref, kbuf, 0, 2, across)
    s_across = token_copy(sbuf.at[rows(0)], sbuf, 1, 2, across)
    k_mate = token_copy(k_ref, kbuf, 0, 1, mate)
    s_mate = token_copy(sbuf.at[rows(0)], sbuf, 1, 1, mate)
    for copy in loads[2:]:
        copy.wait()

    old_sums = []
    for i in range(2):
        old[i * hb : (i + 1) * hb, :] = jnp.transpose(wrows[i, :, cols].astype(F32))
        whole = wrows[i].astype(F32)
        squares = whole * whole
        folded = squares[:, 0:hb]
        for j in range(1, 4):
            folded = folded + squares[:, j * hb : (j + 1) * hb]
        old_sums.append(jnp.sum(jnp.transpose(folded), axis=0, keepdims=True))
    old_out = wback[pl.ds(pl.multiple_of(plane * rb, rb), rb), :].astype(F32)

    def pre(span):
        both = jnp.dot(kbuf[span, :], wcat[...], preferred_element_type=F32)
        gate_pre, up_pre = both[:, 0:hb], both[:, hb : 2 * hb]
        sigma = jax.nn.sigmoid(gate_pre)
        swish = gate_pre * sigma
        act = (swish * up_pre).astype(BF16)
        slope = up_pre * (sigma * (1.0 + gate_pre * (1.0 - sigma)))
        return act, swish, slope

    def grads(span, act, swish, slope):
        back = lax.dot_general(sbuf[span, :], wback[...], NT, preferred_element_type=F32)
        d_gate = (back * slope).astype(BF16)
        d_up = (back * swish).astype(BF16)
        both = jnp.concatenate([d_gate, d_up], axis=1)
        g_in = lax.dot_general(both, kbuf[span, :], TN, preferred_element_type=F32)
        g_out = lax.dot_general(act, sbuf[span, :], TN, preferred_element_type=F32)
        return g_in, g_out

    k_mate.wait_recv()
    s_mate.wait_recv()
    first = slice(0, 2 * tokens)
    g_in, g_out = grads(first, *pre(first))
    acc_in[...] = g_in
    acc_out[...] = g_out

    second = slice(2 * tokens, 4 * tokens)
    k_across.wait_recv()
    k_forward = token_copy(kbuf.at[rows(2)], kbuf, 0, 3, mate)
    k_forward.wait_recv()
    ready = pre(second)
    s_across.wait_recv()
    s_forward = token_copy(sbuf.at[rows(2)], sbuf, 1, 3, mate)
    q_copy = send(q_ref, qbuf.at[rows(1)], q_send, q_recv, across)
    s_forward.wait_recv()
    g_in, g_out = grads(second, *ready)
    acc_in[...] += g_in
    acc_out[...] += g_out

    def part(p):
        top = acc_in[:, pl.ds(pl.multiple_of(p * db, db), db)]
        low = acc_out[pl.ds(pl.multiple_of(p * rb, rb), rb), :]
        return top, low

    g_copies = {}
    for d in (2, 1, 3) if planes == 4 else range(1, planes):
        top, low = part(plane_at(d))
        gsend[d - 1, 0 : 2 * hb, :] = top.astype(BF16)
        for j in range(spread):
            gsend[d - 1, 2 * hb + j * rb : 2 * hb + (j + 1) * rb, :] = low[
                :, j * db : (j + 1) * db
            ].astype(BF16)
        slot = planes - 1 - d
        g_copies[d] = send(
            gsend.at[d - 1], grecv.at[slot], g_send.at[d - 1], g_recv.at[slot], same_spot(d)
        )
    top, low = part(plane)
    sum_top = old[...] + top
    sum_low = [
        old_out[:, j * db : (j + 1) * db] + low[:, j * db : (j + 1) * db] for j in range(spread)
    ]
    for slot in range(planes - 1):
        g_copies[planes - 1 - slot].wait_recv()
        sum_top = sum_top + grecv[slot, 0 : 2 * hb, :].astype(F32)
        for j in range(spread):
            sum_low[j] = sum_low[j] + grecv[
                slot, 2 * hb + j * rb : 2 * hb + (j + 1) * rb, :
            ].astype(F32)

    squares = sum_top * sum_top
    mine = [
        jnp.sum(squares[i * hb : (i + 1) * hb, :], axis=0, keepdims=True) for i in range(2)
    ]
    stat[0] = jnp.concatenate([jnp.broadcast_to(one, (4, db)) for one in mine], axis=0)
    st_copies = [
        send(stat.at[0], stat.at[i + 1], st_send.at[i], st_recv.at[i], peer)
        for i, peer in enumerate((mate, across, diagonal))
    ]

    new_sum = sum(jnp.sum(one * one, axis=1, keepdims=True) for one in sum_low)
    old_sum = jnp.sum(old_out * old_out, axis=1, keepdims=True)
    factor = jnp.sqrt(old_sum / width + epsilon) / jnp.sqrt(new_sum / width + epsilon)
    wbuf[0, plane, 0 : 2 * hb, :] = sum_top.astype(BF16)
    for j in range(spread):
        wbuf[0, plane, 2 * hb + j * rb : 2 * hb + (j + 1) * rb, :] = (
            sum_low[j] * factor
        ).astype(BF16)

    w_copies = {}
    for d in (2, 1, 3) if planes == 4 else range(1, planes):
        slot = planes - 1 - d
        w_copies[d] = send(
            wbuf.at[0, plane], wbuf.at[0, plane], w_send.at[d - 1], w_recv.at[slot], same_spot(d)
        )

    def to_mate(index, p):
        return send(wbuf.at[0, p], wbuf.at[1, p], c_send.at[index], c_recv.at[index], mate)

    c_copies = [to_mate(0, plane)]

    for copy in st_copies:
        copy.wait_recv()
    total = stat[0] + stat[1] + stat[2] + stat[3]
    olds = jnp.concatenate([jnp.broadcast_to(one, (4, db)) for one in old_sums], axis=0)
    fact[plane] = jnp.sqrt(olds / hidden + epsilon) / jnp.sqrt(total / hidden + epsilon)
    f_copies = {}
    for d in range(1, planes):
        slot = planes - 1 - d
        f_copies[d] = send(
            fact.at[plane], fact.at[plane], f_send.at[d - 1], f_recv.at[slot], same_spot(d)
        )

    def arrived(buf, recv_sem, peer, send_sem):
        pltpu.make_async_remote_copy(
            src_ref=buf,
            dst_ref=buf,
            send_sem=send_sem,
            recv_sem=recv_sem,
            device_id=peer,
            device_id_type=MESH,
        ).wait_recv()

    def place(which, p):
        to = pl.ds(pl.multiple_of(p * db, db), db)
        for i in range(2):
            rows_of = slice(i * hb, (i + 1) * hb)
            scaled = wbuf[which, p, rows_of, :].astype(F32) * fact[p, 4 * i : 4 * i + 1, :]
            wq[which * 2 * hb + i * hb : which * 2 * hb + (i + 1) * hb, to] = scaled.astype(BF16)
        for j in range(spread):
            wo[pl.ds(pl.multiple_of(which * hb + p * rb, rb), rb), j * db : (j + 1) * db] = wbuf[
                which, p, 2 * hb + j * rb : 2 * hb + (j + 1) * rb, :
            ]

    place(0, plane)
    arrived(wbuf.at[1, plane], c_recv.at[0], mate, c_send.at[0])
    place(1, plane)
    order = (1, 3, 2) if planes == 4 else tuple(range(1, planes))
    for d in order:
        p = plane_at(d)
        arrived(wbuf.at[0, p], w_recv.at[d - 1], same_spot(d), w_send.at[d - 1])
        c_copies.append(to_mate(d, p))
        arrived(fact.at[p], f_recv.at[d - 1], same_spot(d), f_send.at[d - 1])
        place(0, p)
    q_copy.wait_recv()
    for d in order:
        p = plane_at(d)
        arrived(wbuf.at[1, p], c_recv.at[d], mate, c_send.at[d])
        place(1, p)

    def apply(span):
        pres = lax.dot_general(qbuf[span, :], wq[...], NT, preferred_element_type=F32)
        acts = []
        for which in range(2):
            gate = pres[:, which * 2 * hb : which * 2 * hb + hb]
            up = pres[:, which * 2 * hb + hb : (which + 1) * 2 * hb]
            acts.append((gate * jax.nn.sigmoid(gate) * up).astype(BF16))
        return jnp.dot(jnp.concatenate(acts, axis=1), wo[...], preferred_element_type=F32)

    psend[...] = apply(slice(tokens, 2 * tokens)).astype(BF16)
    p_copy = send(psend, precv, p_send, p_recv, across)
    own = apply(slice(0, tokens))
    p_copy.wait_recv()
    o_ref[...] = (own + precv[...].astype(F32)).astype(BF16)

    outgoing = [k_across, s_across, k_mate, s_mate, k_forward, s_forward, q_copy, p_copy]
    outgoing += list(g_copies.values()) + list(w_copies.values()) + list(f_copies.values())
    outgoing += st_copies + c_copies
    for copy in outgoing:
        copy.wait_send()


def fused(keys, values, queries, learn_rate, w_gate, w_up, w_out):
    tokens, width = keys.shape
    hidden = w_gate.shape[1]
    planes = lax.axis_size("seq") // 2
    hb, db = hidden // 4, width // planes
    part_rows = 3 * hb
    vmem = pltpu.VMEM
    dma = pltpu.SemaphoreType.DMA
    scratch = [
        vmem((4 * tokens, width), BF16),
        vmem((4 * tokens, width), BF16),
        vmem((2 * tokens, width), BF16),
        vmem((width, 2 * hb), BF16),
        vmem((hb, width), BF16),
        vmem((tokens, width), BF16),
        vmem((1, tokens), F32),
        vmem((2, db, hidden), BF16),
        vmem((2 * hb, db), F32),
        vmem((2 * hb, width), F32),
        vmem((hb, width), F32),
        vmem((planes - 1, part_rows, db), BF16),
        vmem((planes - 1, part_rows, db), BF16),
        vmem((4, 8, db), F32),
        vmem((planes, 8, db), F32),
        vmem((2, planes, part_rows, db), BF16),
        vmem((4 * hb, width), BF16),
        vmem((2 * hb, width), BF16),
        vmem((tokens, width), BF16),
        vmem((tokens, width), BF16),
        dma((2, 3)),
        dma((2, 3)),
        dma,
        dma,
        dma((planes - 1,)),
        dma((planes - 1,)),
        dma((3,)),
        dma((3,)),
        dma((planes - 1,)),
        dma((planes - 1,)),
        dma((planes - 1,)),
        dma((planes - 1,)),
        dma((planes,)),
        dma((planes,)),
        dma,
        dma,
        dma((9,)),
    ]
    return pl.pallas_call(
        functools.partial(kernel, planes),
        out_shape=jax.ShapeDtypeStruct((tokens, width), BF16),
        in_specs=[pl.BlockSpec(memory_space=pltpu.HBM)] * 7,
        out_specs=pl.BlockSpec(memory_space=pltpu.VMEM),
        scratch_shapes=scratch,
        compiler_params=pltpu.CompilerParams(
            collective_id=0, has_side_effects=True, vmem_limit_bytes=40 * 2**20
        ),
        cost_estimate=pl.CostEstimate(
            flops=2 * tokens * width * hidden * 9, bytes_accessed=2 * 2**20, transcendentals=0
        ),
    )(learn_rate.reshape(1, tokens), keys, values, queries, w_gate, w_up, w_out)


def renorm(weight, grads):
    old = weight.astype(F32)
    update = old + grads
    factor = jnp.sqrt(jnp.mean(old * old, axis=1, keepdims=True) + epsilon) / jnp.sqrt(
        jnp.mean(update * update, axis=1, keepdims=True) + epsilon
    )
    return (update * factor).astype(BF16)


def plain(keys, values, queries, learn_rate, w_gate, w_up, w_out):
    hidden = w_gate.shape[1]
    axes = ("seq", "outer")
    shards = lax.axis_size(axes)
    rows_in, rows_out = w_gate.shape[0] // shards, w_out.shape[0] // shards
    position = lax.axis_index(axes)
    scaled = (learn_rate[:, None] * values.astype(F32)).astype(BF16)
    gate_pre = jnp.dot(keys, w_gate, preferred_element_type=F32)
    up_pre = jnp.dot(keys, w_up, preferred_element_type=F32)
    back = lax.dot_general(scaled, w_out, NT, preferred_element_type=F32)
    activation = (jax.nn.silu(gate_pre) * up_pre).astype(BF16)
    d_gate = (back * up_pre * silu_grad(gate_pre)).astype(BF16)
    d_up = (back * jax.nn.silu(gate_pre)).astype(BF16)
    both = jnp.concatenate([d_gate, d_up], axis=1)
    full_in = lax.dot_general(keys, both, TN, preferred_element_type=F32)
    full_out = lax.dot_general(activation, scaled, TN, preferred_element_type=F32)
    grad_in = lax.psum_scatter(full_in, axes, scatter_dimension=0, tiled=True)
    grad_out = lax.psum_scatter(full_out, axes, scatter_dimension=0, tiled=True)
    own_gate = lax.dynamic_slice_in_dim(w_gate, position * rows_in, rows_in, 0)
    own_up = lax.dynamic_slice_in_dim(w_up, position * rows_in, rows_in, 0)
    own_out = lax.dynamic_slice_in_dim(w_out, position * rows_out, rows_out, 0)
    news = (
        renorm(own_gate, grad_in[:, :hidden]),
        renorm(own_up, grad_in[:, hidden:]),
        renorm(own_out, grad_out),
    )
    gate, up, out = [lax.all_gather(new, axes, axis=0, tiled=True) for new in news]
    q_gate = jnp.dot(queries, gate, preferred_element_type=F32)
    q_up = jnp.dot(queries, up, preferred_element_type=F32)
    q_act = (jax.nn.silu(q_gate) * q_up).astype(BF16)
    return jnp.dot(q_act, out, preferred_element_type=F32).astype(BF16)


def local(keys, values, queries, learn_rate, w_gate, w_up, w_out):
    width, hidden = w_gate.shape
    tokens = keys.shape[0]
    seq, cores = lax.axis_size("seq"), lax.axis_size("outer")
    planes = seq // 2
    fits = (
        cores == 2
        and seq % 2 == 0
        and planes > 1
        and width % (128 * planes) == 0
        and hidden % (4 * 32 * planes) == 0
        and hidden // 4 == 128
        and tokens == 128
    )
    chosen = fused if fits else plain
    return chosen(keys, values, queries, learn_rate, w_gate, w_up, w_out)


def solution(mesh):
    placed = (
        P(("grp", "seq", "outer"), None),
        P(("grp", "seq", "outer"), None),
        P(("grp", "seq", "outer"), None),
        P(("grp", "seq", "outer")),
        P("grp", None),
        P("grp", None),
        P("grp", None),
    )
    return jax.shard_map(
        local,
        mesh=mesh,
        in_specs=placed,
        out_specs=P(("grp", "seq", "outer"), None),
        check_vma=False,
    )
```

```python
import functools

import jax
import jax.numpy as jnp
from jax import lax
from jax.experimental import pallas as pl
from jax.experimental.pallas import tpu as pltpu
from jax.sharding import PartitionSpec as P

epsilon = 1e-06
MESH = pl.DeviceIdType.MESH
F32 = jnp.float32
BF16 = jnp.bfloat16
NT = (((1,), (1,)), ((), ()))
TN = (((0,), (0,)), ((), ()))


def silu_grad(inputs):
    sigma = jax.nn.sigmoid(inputs)
    return sigma * (1.0 + inputs * (1.0 - sigma))


def kernel(
    planes,
    lr_ref,
    k_ref,
    v_ref,
    q_ref,
    wg_ref,
    wu_ref,
    wo_ref,
    o_ref,
    kbuf,
    sbuf,
    qbuf,
    wcat,
    wback,
    vbuf,
    lrbuf,
    wrows,
    old,
    acc_in,
    acc_out,
    gsend,
    grecv,
    stat,
    fact,
    wbuf,
    wq,
    wo,
    psend,
    precv,
    tok_send,
    tok_recv,
    q_send,
    q_recv,
    g_send,
    g_recv,
    st_send,
    st_recv,
    f_send,
    f_recv,
    w_send,
    w_recv,
    c_send,
    c_recv,
    p_send,
    p_recv,
    load,
):
    tokens, width = k_ref.shape
    hidden = wg_ref.shape[1]
    hb = hidden // 4
    db = width // planes
    rb = hb // planes
    spread = width // db
    seq = lax.axis_index("seq")
    core = lax.axis_index("outer")
    plane, side = seq // 2, seq % 2
    quarter = side * 2 + core
    cols = pl.ds(pl.multiple_of(quarter * hb, hb), hb)

    mate = {"outer": 1 - core}
    across = {"seq": plane * 2 + 1 - side}
    diagonal = {"seq": plane * 2 + 1 - side, "outer": 1 - core}

    def plane_at(distance):
        return (plane + distance) % planes

    def same_spot(distance):
        return {"seq": plane_at(distance) * 2 + side}

    def rows(slot):
        return pl.ds(slot * tokens, tokens)

    my_cols = pl.ds(pl.multiple_of(plane * db, db), db)
    moves = (
        (lr_ref, lrbuf),
        (v_ref, vbuf),
        (k_ref, kbuf.at[rows(0)]),
        (wg_ref.at[:, cols], wcat.at[:, 0:hb]),
        (wu_ref.at[:, cols], wcat.at[:, hb : 2 * hb]),
        (wo_ref.at[cols], wback),
        (wg_ref.at[my_cols], wrows.at[0]),
        (wu_ref.at[my_cols], wrows.at[1]),
        (q_ref, qbuf.at[rows(0)]),
    )
    loads = [pltpu.make_async_copy(a, b, load.at[i]) for i, (a, b) in enumerate(moves)]
    for copy in loads:
        copy.start()

    barrier = pltpu.get_barrier_semaphore()
    peers = [mate, across, diagonal] + [same_spot(d) for d in range(1, planes)]
    for peer in peers:
        pl.semaphore_signal(barrier, inc=1, device_id=peer, device_id_type=MESH)

    loads[0].wait()
    loads[1].wait()
    lr_cols = jnp.transpose(jnp.broadcast_to(lrbuf[...], (tokens, tokens)))
    rate = lr_cols[:, 0:1]
    sbuf[rows(0), :] = (rate * vbuf[...].astype(F32)).astype(BF16)
    pl.semaphore_wait(barrier, len(peers))

    def send(src, dst, send_sem, recv_sem, peer):
        copy = pltpu.make_async_remote_copy(
            src_ref=src,
            dst_ref=dst,
            send_sem=send_sem,
            recv_sem=recv_sem,
            device_id=peer,
            device_id_type=MESH,
        )
        copy.start()
        return copy

    def token_copy(src, buf, kind, dst_slot, peer):
        return send(
            src,
            buf.at[rows(dst_slot)],
            tok_send.at[kind, dst_slot - 1],
            tok_recv.at[kind, dst_slot - 1],
            peer,
        )

    k_across = token_copy(k_ref, kbuf, 0, 2, across)
    s_across = token_copy(sbuf.at[rows(0)], sbuf, 1, 2, across)
    k_mate = token_copy(k_ref, kbuf, 0, 1, mate)
    s_mate = token_copy(sbuf.at[rows(0)], sbuf, 1, 1, mate)
    for copy in loads[2:]:
        copy.wait()

    old_sums = []
    for i in range(2):
        old[i * hb : (i + 1) * hb, :] = jnp.transpose(wrows[i, :, cols].astype(F32))
        whole = wrows[i].astype(F32)
        squares = whole * whole
        folded = squares[:, 0:hb]
        for j in range(1, 4):
            folded = folded + squares[:, j * hb : (j + 1) * hb]
        old_sums.append(jnp.sum(jnp.transpose(folded), axis=0, keepdims=True))
    old_out = wback[pl.ds(pl.multiple_of(plane * rb, rb), rb), :].astype(F32)

    def pre(span):
        both = jnp.dot(kbuf[span, :], wcat[...], preferred_element_type=F32)
        gate_pre, up_pre = both[:, 0:hb], both[:, hb : 2 * hb]
        sigma = jax.nn.sigmoid(gate_pre)
        swish = gate_pre * sigma
        act = (swish * up_pre).astype(BF16)
        slope = up_pre * (sigma * (1.0 + gate_pre * (1.0 - sigma)))
        return act, swish, slope

    def grads(span, act, swish, slope):
        back = lax.dot_general(sbuf[span, :], wback[...], NT, preferred_element_type=F32)
        d_gate = (back * slope).astype(BF16)
        d_up = (back * swish).astype(BF16)
        both = jnp.concatenate([d_gate, d_up], axis=1)
        g_in = lax.dot_general(both, kbuf[span, :], TN, preferred_element_type=F32)
        g_out = lax.dot_general(act, sbuf[span, :], TN, preferred_element_type=F32)
        return g_in, g_out

    k_mate.wait_recv()
    s_mate.wait_recv()
    first = slice(0, 2 * tokens)
    g_in, g_out = grads(first, *pre(first))
    acc_in[...] = g_in
    acc_out[...] = g_out

    second = slice(2 * tokens, 4 * tokens)
    k_across.wait_recv()
    k_forward = token_copy(kbuf.at[rows(2)], kbuf, 0, 3, mate)
    k_forward.wait_recv()
    ready = pre(second)
    s_across.wait_recv()
    s_forward = token_copy(sbuf.at[rows(2)], sbuf, 1, 3, mate)
    q_copy = send(q_ref, qbuf.at[rows(1)], q_send, q_recv, across)
    s_forward.wait_recv()
    g_in, g_out = grads(second, *ready)
    acc_in[...] += g_in
    acc_out[...] += g_out

    def part(p):
        top = acc_in[:, pl.ds(pl.multiple_of(p * db, db), db)]
        low = acc_out[pl.ds(pl.multiple_of(p * rb, rb), rb), :]
        return top, low

    g_copies = {}
    for d in (2, 1, 3) if planes == 4 else range(1, planes):
        top, low = part(plane_at(d))
        gsend[d - 1, 0 : 2 * hb, :] = top.astype(BF16)
        for j in range(spread):
            gsend[d - 1, 2 * hb + j * rb : 2 * hb + (j + 1) * rb, :] = low[
                :, j * db : (j + 1) * db
            ].astype(BF16)
        slot = planes - 1 - d
        g_copies[d] = send(
            gsend.at[d - 1], grecv.at[slot], g_send.at[d - 1], g_recv.at[slot], same_spot(d)
        )
    top, low = part(plane)
    sum_top = old[...] + top
    sum_low = [
        old_out[:, j * db : (j + 1) * db] + low[:, j * db : (j + 1) * db] for j in range(spread)
    ]
    for slot in range(planes - 1):
        g_copies[planes - 1 - slot].wait_recv()
        sum_top = sum_top + grecv[slot, 0 : 2 * hb, :].astype(F32)
        for j in range(spread):
            sum_low[j] = sum_low[j] + grecv[
                slot, 2 * hb + j * rb : 2 * hb + (j + 1) * rb, :
            ].astype(F32)

    squares = sum_top * sum_top
    mine = [
        jnp.sum(squares[i * hb : (i + 1) * hb, :], axis=0, keepdims=True) for i in range(2)
    ]
    stat[0] = jnp.concatenate([jnp.broadcast_to(one, (4, db)) for one in mine], axis=0)
    st_copies = [
        send(stat.at[0], stat.at[i + 1], st_send.at[i], st_recv.at[i], peer)
        for i, peer in enumerate((mate, across, diagonal))
    ]

    new_sum = sum(jnp.sum(one * one, axis=1, keepdims=True) for one in sum_low)
    old_sum = jnp.sum(old_out * old_out, axis=1, keepdims=True)
    factor = jnp.sqrt(old_sum / width + epsilon) / jnp.sqrt(new_sum / width + epsilon)
    wbuf[0, plane, 0 : 2 * hb, :] = sum_top.astype(BF16)
    for j in range(spread):
        wbuf[0, plane, 2 * hb + j * rb : 2 * hb + (j + 1) * rb, :] = (
            sum_low[j] * factor
        ).astype(BF16)

    w_copies = {}
    for d in (2, 1, 3) if planes == 4 else range(1, planes):
        slot = planes - 1 - d
        w_copies[d] = send(
            wbuf.at[0, plane], wbuf.at[0, plane], w_send.at[d - 1], w_recv.at[slot], same_spot(d)
        )

    def to_mate(index, p):
        return send(wbuf.at[0, p], wbuf.at[1, p], c_send.at[index], c_recv.at[index], mate)

    c_copies = [to_mate(0, plane)]

    for copy in st_copies:
        copy.wait_recv()
    total = stat[0] + stat[1] + stat[2] + stat[3]
    olds = jnp.concatenate([jnp.broadcast_to(one, (4, db)) for one in old_sums], axis=0)
    fact[plane] = jnp.sqrt(olds / hidden + epsilon) / jnp.sqrt(total / hidden + epsilon)
    f_copies = {}
    for d in range(1, planes):
        slot = planes - 1 - d
        f_copies[d] = send(
            fact.at[plane], fact.at[plane], f_send.at[d - 1], f_recv.at[slot], same_spot(d)
        )

    def arrived(buf, recv_sem, peer, send_sem):
        pltpu.make_async_remote_copy(
            src_ref=buf,
            dst_ref=buf,
            send_sem=send_sem,
            recv_sem=recv_sem,
            device_id=peer,
            device_id_type=MESH,
        ).wait_recv()

    def place(which, p):
        to = pl.ds(pl.multiple_of(p * db, db), db)
        for i in range(2):
            rows_of = slice(i * hb, (i + 1) * hb)
            scaled = wbuf[which, p, rows_of, :].astype(F32) * fact[p, 4 * i : 4 * i + 1, :]
            wq[which * 2 * hb + i * hb : which * 2 * hb + (i + 1) * hb, to] = scaled.astype(BF16)
        for j in range(spread):
            wo[pl.ds(pl.multiple_of(which * hb + p * rb, rb), rb), j * db : (j + 1) * db] = wbuf[
                which, p, 2 * hb + j * rb : 2 * hb + (j + 1) * rb, :
            ]

    place(0, plane)
    arrived(wbuf.at[1, plane], c_recv.at[0], mate, c_send.at[0])
    place(1, plane)
    order = (1, 3, 2) if planes == 4 else tuple(range(1, planes))
    for d in order:
        p = plane_at(d)
        arrived(wbuf.at[0, p], w_recv.at[d - 1], same_spot(d), w_send.at[d - 1])
        c_copies.append(to_mate(d, p))
        arrived(fact.at[p], f_recv.at[d - 1], same_spot(d), f_send.at[d - 1])
        place(0, p)
    q_copy.wait_recv()
    for d in order:
        p = plane_at(d)
        arrived(wbuf.at[1, p], c_recv.at[d], mate, c_send.at[d])
        place(1, p)

    def apply(span):
        pres = lax.dot_general(qbuf[span, :], wq[...], NT, preferred_element_type=F32)
        acts = []
        for which in range(2):
            gate = pres[:, which * 2 * hb : which * 2 * hb + hb]
            up = pres[:, which * 2 * hb + hb : (which + 1) * 2 * hb]
            acts.append((gate * jax.nn.sigmoid(gate) * up).astype(BF16))
        return jnp.dot(jnp.concatenate(acts, axis=1), wo[...], preferred_element_type=F32)

    psend[...] = apply(slice(tokens, 2 * tokens)).astype(BF16)
    p_copy = send(psend, precv, p_send, p_recv, across)
    own = apply(slice(0, tokens))
    p_copy.wait_recv()
    o_ref[...] = (own + precv[...].astype(F32)).astype(BF16)

    outgoing = [k_across, s_across, k_mate, s_mate, k_forward, s_forward, q_copy, p_copy]
    outgoing += list(g_copies.values()) + list(w_copies.values()) + list(f_copies.values())
    outgoing += st_copies + c_copies
    for copy in outgoing:
        copy.wait_send()


def fused(keys, values, queries, learn_rate, w_gate, w_up, w_out):
    tokens, width = keys.shape
    hidden = w_gate.shape[1]
    planes = lax.axis_size("seq") // 2
    hb, db = hidden // 4, width // planes
    part_rows = 3 * hb
    vmem = pltpu.VMEM
    dma = pltpu.SemaphoreType.DMA
    scratch = [
        vmem((4 * tokens, width), BF16),
        vmem((4 * tokens, width), BF16),
        vmem((2 * tokens, width), BF16),
        vmem((width, 2 * hb), BF16),
        vmem((hb, width), BF16),
        vmem((tokens, width), BF16),
        vmem((1, tokens), F32),
        vmem((2, db, hidden), BF16),
        vmem((2 * hb, db), F32),
        vmem((2 * hb, width), F32),
        vmem((hb, width), F32),
        vmem((planes - 1, part_rows, db), BF16),
        vmem((planes - 1, part_rows, db), BF16),
        vmem((4, 8, db), F32),
        vmem((planes, 8, db), F32),
        vmem((2, planes, part_rows, db), BF16),
        vmem((4 * hb, width), BF16),
        vmem((2 * hb, width), BF16),
        vmem((tokens, width), BF16),
        vmem((tokens, width), BF16),
        dma((2, 3)),
        dma((2, 3)),
        dma,
        dma,
        dma((planes - 1,)),
        dma((planes - 1,)),
        dma((3,)),
        dma((3,)),
        dma((planes - 1,)),
        dma((planes - 1,)),
        dma((planes - 1,)),
        dma((planes - 1,)),
        dma((planes,)),
        dma((planes,)),
        dma,
        dma,
        dma((9,)),
    ]
    return pl.pallas_call(
        functools.partial(kernel, planes),
        out_shape=jax.ShapeDtypeStruct((tokens, width), BF16),
        in_specs=[pl.BlockSpec(memory_space=pltpu.HBM)] * 7,
        out_specs=pl.BlockSpec(memory_space=pltpu.VMEM),
        scratch_shapes=scratch,
        compiler_params=pltpu.CompilerParams(
            collective_id=0, has_side_effects=True, vmem_limit_bytes=60 * 2**20
        ),
        cost_estimate=pl.CostEstimate(
            flops=2 * tokens * width * hidden * 9, bytes_accessed=2 * 2**20, transcendentals=0
        ),
    )(learn_rate.reshape(1, tokens), keys, values, queries, w_gate, w_up, w_out)


def renorm(weight, grads):
    old = weight.astype(F32)
    update = old + grads
    factor = jnp.sqrt(jnp.mean(old * old, axis=1, keepdims=True) + epsilon) / jnp.sqrt(
        jnp.mean(update * update, axis=1, keepdims=True) + epsilon
    )
    return (update * factor).astype(BF16)


def plain(keys, values, queries, learn_rate, w_gate, w_up, w_out):
    hidden = w_gate.shape[1]
    axes = ("seq", "outer")
    shards = lax.axis_size(axes)
    rows_in, rows_out = w_gate.shape[0] // shards, w_out.shape[0] // shards
    position = lax.axis_index(axes)
    scaled = (learn_rate[:, None] * values.astype(F32)).astype(BF16)
    gate_pre = jnp.dot(keys, w_gate, preferred_element_type=F32)
    up_pre = jnp.dot(keys, w_up, preferred_element_type=F32)
    back = lax.dot_general(scaled, w_out, NT, preferred_element_type=F32)
    activation = (jax.nn.silu(gate_pre) * up_pre).astype(BF16)
    d_gate = (back * up_pre * silu_grad(gate_pre)).astype(BF16)
    d_up = (back * jax.nn.silu(gate_pre)).astype(BF16)
    both = jnp.concatenate([d_gate, d_up], axis=1)
    full_in = lax.dot_general(keys, both, TN, preferred_element_type=F32)
    full_out = lax.dot_general(activation, scaled, TN, preferred_element_type=F32)
    grad_in = lax.psum_scatter(full_in, axes, scatter_dimension=0, tiled=True)
    grad_out = lax.psum_scatter(full_out, axes, scatter_dimension=0, tiled=True)
    own_gate = lax.dynamic_slice_in_dim(w_gate, position * rows_in, rows_in, 0)
    own_up = lax.dynamic_slice_in_dim(w_up, position * rows_in, rows_in, 0)
    own_out = lax.dynamic_slice_in_dim(w_out, position * rows_out, rows_out, 0)
    news = (
        renorm(own_gate, grad_in[:, :hidden]),
        renorm(own_up, grad_in[:, hidden:]),
        renorm(own_out, grad_out),
    )
    gate, up, out = [lax.all_gather(new, axes, axis=0, tiled=True) for new in news]
    q_gate = jnp.dot(queries, gate, preferred_element_type=F32)
    q_up = jnp.dot(queries, up, preferred_element_type=F32)
    q_act = (jax.nn.silu(q_gate) * q_up).astype(BF16)
    return jnp.dot(q_act, out, preferred_element_type=F32).astype(BF16)


def local(keys, values, queries, learn_rate, w_gate, w_up, w_out):
    width, hidden = w_gate.shape
    tokens = keys.shape[0]
    seq, cores = lax.axis_size("seq"), lax.axis_size("outer")
    planes = seq // 2
    fits = (
        cores == 2
        and seq % 2 == 0
        and planes > 1
        and width % (128 * planes) == 0
        and hidden % (4 * 32 * planes) == 0
        and hidden // 4 == 128
        and tokens == 128
    )
    chosen = fused if fits else plain
    return chosen(keys, values, queries, learn_rate, w_gate, w_up, w_out)


def solution(mesh):
    placed = (
        P(("grp", "seq", "outer"), None),
        P(("grp", "seq", "outer"), None),
        P(("grp", "seq", "outer"), None),
        P(("grp", "seq", "outer")),
        P("grp", None),
        P("grp", None),
        P("grp", None),
    )
    return jax.shard_map(
        local,
        mesh=mesh,
        in_specs=placed,
        out_specs=P(("grp", "seq", "outer"), None),
        check_vma=False,
    )
```

```python
import functools

import jax
import jax.numpy as jnp
from jax import lax
from jax.experimental import pallas as pl
from jax.experimental.pallas import tpu as pltpu
from jax.sharding import PartitionSpec as P

epsilon = 1e-06
MESH = pl.DeviceIdType.MESH
F32 = jnp.float32
BF16 = jnp.bfloat16
NT = (((1,), (1,)), ((), ()))
TN = (((0,), (0,)), ((), ()))


def silu_grad(inputs):
    sigma = jax.nn.sigmoid(inputs)
    return sigma * (1.0 + inputs * (1.0 - sigma))


def kernel(
    planes,
    lr_ref,
    k_ref,
    v_ref,
    q_ref,
    wg_ref,
    wu_ref,
    wo_ref,
    o_ref,
    kbuf,
    sbuf,
    qbuf,
    wcat,
    wback,
    vbuf,
    lrbuf,
    wrows,
    old,
    update,
    acc_in,
    acc_out,
    gsend,
    grecv,
    stat,
    fact,
    wbuf,
    wq,
    wo,
    psend,
    precv,
    tok_send,
    tok_recv,
    q_send,
    q_recv,
    g_send,
    g_recv,
    st_send,
    st_recv,
    f_send,
    f_recv,
    w_send,
    w_recv,
    c_send,
    c_recv,
    p_send,
    p_recv,
    load,
):
    tokens, width = k_ref.shape
    hidden = wg_ref.shape[1]
    hb = hidden // 4
    db = width // planes
    rb = hb // planes
    spread = width // db
    seq = lax.axis_index("seq")
    core = lax.axis_index("outer")
    plane, side = seq // 2, seq % 2
    quarter = side * 2 + core
    cols = pl.ds(pl.multiple_of(quarter * hb, hb), hb)

    inner = jnp.logical_or(plane == 1, plane == 2)
    outer = jnp.logical_not(inner)
    low_half = plane < 2
    buddy = jnp.where(low_half, 1 - plane, 5 - plane)
    fin = jnp.where(low_half, 2, 1)
    far = jnp.where(low_half, 3, 0)

    mate = {"outer": 1 - core}
    across = {"seq": plane * 2 + 1 - side}
    diagonal = {"seq": plane * 2 + 1 - side, "outer": 1 - core}

    def plane_at(distance):
        return (plane + distance) % planes

    def same_spot(distance):
        return {"seq": plane_at(distance) * 2 + side}

    def rows(slot):
        return pl.ds(slot * tokens, tokens)

    my_cols = pl.ds(pl.multiple_of(plane * db, db), db)
    moves = (
        (lr_ref, lrbuf),
        (v_ref, vbuf),
        (k_ref, kbuf.at[rows(0)]),
        (wg_ref.at[:, cols], wcat.at[:, 0:hb]),
        (wu_ref.at[:, cols], wcat.at[:, hb : 2 * hb]),
        (wo_ref.at[cols], wback),
        (wg_ref.at[my_cols], wrows.at[0]),
        (wu_ref.at[my_cols], wrows.at[1]),
        (q_ref, qbuf.at[rows(0)]),
    )
    loads = [pltpu.make_async_copy(a, b, load.at[i]) for i, (a, b) in enumerate(moves)]
    for copy in loads:
        copy.start()

    barrier = pltpu.get_barrier_semaphore()
    peers = [mate, across, diagonal] + [same_spot(d) for d in range(1, planes)]
    for peer in peers:
        pl.semaphore_signal(barrier, inc=1, device_id=peer, device_id_type=MESH)

    loads[0].wait()
    loads[1].wait()
    lr_cols = jnp.transpose(jnp.broadcast_to(lrbuf[...], (tokens, tokens)))
    rate = lr_cols[:, 0:1]
    sbuf[rows(0), :] = (rate * vbuf[...].astype(F32)).astype(BF16)
    pl.semaphore_wait(barrier, len(peers))

    def send(src, dst, send_sem, recv_sem, peer):
        copy = pltpu.make_async_remote_copy(
            src_ref=src,
            dst_ref=dst,
            send_sem=send_sem,
            recv_sem=recv_sem,
            device_id=peer,
            device_id_type=MESH,
        )
        copy.start()
        return copy

    def arrived(buf, recv_sem, peer, send_sem):
        pltpu.make_async_remote_copy(
            src_ref=buf,
            dst_ref=buf,
            send_sem=send_sem,
            recv_sem=recv_sem,
            device_id=peer,
            device_id_type=MESH,
        ).wait_recv()

    def token_copy(src, buf, kind, dst_slot, peer):
        return send(
            src,
            buf.at[rows(dst_slot)],
            tok_send.at[kind, dst_slot - 1],
            tok_recv.at[kind, dst_slot - 1],
            peer,
        )

    k_across = token_copy(k_ref, kbuf, 0, 2, across)
    s_across = token_copy(sbuf.at[rows(0)], sbuf, 1, 2, across)
    k_mate = token_copy(k_ref, kbuf, 0, 1, mate)
    s_mate = token_copy(sbuf.at[rows(0)], sbuf, 1, 1, mate)
    for copy in loads[2:]:
        copy.wait()

    old_sums = []
    for i in range(2):
        old[i * hb : (i + 1) * hb, :] = jnp.transpose(wrows[i, :, cols].astype(F32))
        whole = wrows[i].astype(F32)
        squares = whole * whole
        folded = squares[:, 0:hb]
        for j in range(1, 4):
            folded = folded + squares[:, j * hb : (j + 1) * hb]
        old_sums.append(jnp.sum(jnp.transpose(folded), axis=0, keepdims=True))
    old_out = wback[pl.ds(pl.multiple_of(plane * rb, rb), rb), :].astype(F32)
    for j in range(spread):
        old[2 * hb + j * rb : 2 * hb + (j + 1) * rb, :] = old_out[:, j * db : (j + 1) * db]

    def pre(span):
        both = jnp.dot(kbuf[span, :], wcat[...], preferred_element_type=F32)
        gate_pre, up_pre = both[:, 0:hb], both[:, hb : 2 * hb]
        sigma = jax.nn.sigmoid(gate_pre)
        swish = gate_pre * sigma
        act = (swish * up_pre).astype(BF16)
        slope = up_pre * (sigma * (1.0 + gate_pre * (1.0 - sigma)))
        return act, swish, slope

    def grads(span, act, swish, slope):
        back = lax.dot_general(sbuf[span, :], wback[...], NT, preferred_element_type=F32)
        d_gate = (back * slope).astype(BF16)
        d_up = (back * swish).astype(BF16)
        both = jnp.concatenate([d_gate, d_up], axis=1)
        g_in = lax.dot_general(both, kbuf[span, :], TN, preferred_element_type=F32)
        g_out = lax.dot_general(act, sbuf[span, :], TN, preferred_element_type=F32)
        return g_in, g_out

    k_mate.wait_recv()
    s_mate.wait_recv()
    first = slice(0, 2 * tokens)
    g_in, g_out = grads(first, *pre(first))
    acc_in[...] = g_in
    acc_out[...] = g_out

    k_across.wait_recv()
    k_forward = token_copy(kbuf.at[rows(2)], kbuf, 0, 3, mate)
    ready = pre(rows(2))
    k_forward.wait_recv()
    last = pre(rows(3))
    s_across.wait_recv()
    s_forward = token_copy(sbuf.at[rows(2)], sbuf, 1, 3, mate)
    q_copy = send(q_ref, qbuf.at[rows(1)], q_send, q_recv, across)
    g_in, g_out = grads(rows(2), *ready)
    acc_in[...] += g_in
    acc_out[...] += g_out
    s_forward.wait_recv()
    g_in, g_out = grads(rows(3), *last)
    acc_in[...] += g_in
    acc_out[...] += g_out

    def part(p):
        return acc_in[:, pl.ds(pl.multiple_of(p * db, db), db)], acc_out[
            pl.ds(pl.multiple_of(p * rb, rb), rb), :
        ]

    def stacked(p):
        top, low = part(p)
        return jnp.concatenate(
            [top] + [low[:, j * db : (j + 1) * db] for j in range(spread)], axis=0
        )

    def g_copy(i, dst, slot):
        return send(
            gsend.at[i], grecv.at[slot], g_send.at[i], g_recv.at[slot], {"seq": dst * 2 + side}
        )

    def g_arrived(slot):
        arrived(grecv.at[slot], g_recv.at[slot], mate, g_send.at[0])

    gsend[0] = stacked(jnp.where(outer, far, fin)).astype(BF16)
    g_copies = [g_copy(0, jnp.where(outer, buddy, fin), jnp.where(outer, 3, 0))]
    gsend[1] = stacked(jnp.where(outer, fin, buddy)).astype(BF16)
    g_copies.append(g_copy(1, jnp.where(outer, fin, buddy), jnp.where(outer, 1, 0)))

    @pl.when(outer)
    def _():
        gsend[2] = stacked(buddy).astype(BF16)

    @pl.when(inner)
    def _():
        g_arrived(3)
        gsend[2] = (stacked(far) + grecv[3].astype(F32)).astype(BF16)

    g_copies.append(g_copy(2, jnp.where(outer, buddy, far), jnp.where(outer, 2, 1)))
    update[...] = old[...] + stacked(plane)
    g_arrived(0)
    update[...] += grecv[0].astype(F32)

    @pl.when(inner)
    def _():
        g_arrived(2)
        update[...] += grecv[2].astype(F32)

    g_arrived(1)
    update[...] += grecv[1].astype(F32)
    sum_top = update[0 : 2 * hb, :]
    sum_low = [update[2 * hb + j * rb : 2 * hb + (j + 1) * rb, :] for j in range(spread)]

    squares = sum_top * sum_top
    mine = [
        jnp.sum(squares[i * hb : (i + 1) * hb, :], axis=0, keepdims=True) for i in range(2)
    ]
    stat[0] = jnp.concatenate([jnp.broadcast_to(one, (4, db)) for one in mine], axis=0)
    st_copies = [
        send(stat.at[0], stat.at[i + 1], st_send.at[i], st_recv.at[i], peer)
        for i, peer in enumerate((mate, across, diagonal))
    ]

    new_sum = sum(jnp.sum(one * one, axis=1, keepdims=True) for one in sum_low)
    old_sum = jnp.sum(old_out * old_out, axis=1, keepdims=True)
    factor = jnp.sqrt(old_sum / width + epsilon) / jnp.sqrt(new_sum / width + epsilon)
    wbuf[0, plane, 0 : 2 * hb, :] = sum_top.astype(BF16)
    for j in range(spread):
        wbuf[0, plane, 2 * hb + j * rb : 2 * hb + (j + 1) * rb, :] = (
            sum_low[j] * factor
        ).astype(BF16)

    def w_copy(i, p, dst):
        return send(
            wbuf.at[0, p], wbuf.at[0, p], w_send.at[i], w_recv.at[p], {"seq": dst * 2 + side}
        )

    w_copies = [w_copy(0, plane, jnp.where(outer, fin, buddy))]

    def to_mate(index, p):
        return send(wbuf.at[0, p], wbuf.at[1, p], c_send.at[index], c_recv.at[index], mate)

    c_copies = [to_mate(0, plane)]

    for copy in st_copies:
        copy.wait_recv()
    w_copies.append(w_copy(1, plane, jnp.where(outer, buddy, far)))

    @pl.when(inner)
    def _():
        w_copy(2, plane, fin)

    total = stat[0] + stat[1] + stat[2] + stat[3]
    olds = jnp.concatenate([jnp.broadcast_to(one, (4, db)) for one in old_sums], axis=0)
    fact[plane] = jnp.sqrt(olds / hidden + epsilon) / jnp.sqrt(total / hidden + epsilon)
    f_copies = {}
    for d in range(1, planes):
        f_copies[d] = send(
            fact.at[plane], fact.at[plane], f_send.at[d - 1], f_recv.at[plane], same_spot(d)
        )

    def place(which, p):
        to = pl.ds(pl.multiple_of(p * db, db), db)
        for i in range(2):
            rows_of = slice(i * hb, (i + 1) * hb)
            scaled = wbuf[which, p, rows_of, :].astype(F32) * fact[p, 4 * i : 4 * i + 1, :]
            wq[which * 2 * hb + i * hb : which * 2 * hb + (i + 1) * hb, to] = scaled.astype(BF16)
        for j in range(spread):
            wo[pl.ds(pl.multiple_of(which * hb + p * rb, rb), rb), j * db : (j + 1) * db] = wbuf[
                which, p, 2 * hb + j * rb : 2 * hb + (j + 1) * rb, :
            ]

    place(0, plane)
    arrived(wbuf.at[1, plane], c_recv.at[0], mate, c_send.at[0])
    place(1, plane)
    order = (
        jnp.where(outer, buddy, far),
        jnp.where(outer, fin, buddy),
        jnp.where(outer, far, fin),
    )
    for i, p in enumerate(order):
        arrived(wbuf.at[0, p], w_recv.at[p], mate, w_send.at[0])
        c_copies.append(to_mate(i + 1, p))
        if i == 0:

            @pl.when(inner)
            def _():
                w_copy(3, far, buddy)

        arrived(fact.at[p], f_recv.at[p], mate, f_send.at[0])
        place(0, p)
    q_copy.wait_recv()
    for i, p in enumerate(order):
        arrived(wbuf.at[1, p], c_recv.at[i + 1], mate, c_send.at[0])
        place(1, p)

    def apply(span):
        pres = lax.dot_general(qbuf[span, :], wq[...], NT, preferred_element_type=F32)
        acts = []
        for which in range(2):
            gate = pres[:, which * 2 * hb : which * 2 * hb + hb]
            up = pres[:, which * 2 * hb + hb : (which + 1) * 2 * hb]
            acts.append((gate * jax.nn.sigmoid(gate) * up).astype(BF16))
        return jnp.dot(jnp.concatenate(acts, axis=1), wo[...], preferred_element_type=F32)

    psend[...] = apply(slice(tokens, 2 * tokens)).astype(BF16)
    p_copy = send(psend, precv, p_send, p_recv, across)
    own = apply(slice(0, tokens))
    p_copy.wait_recv()
    o_ref[...] = (own + precv[...].astype(F32)).astype(BF16)

    outgoing = [k_across, s_across, k_mate, s_mate, k_forward, s_forward, q_copy, p_copy]
    outgoing += g_copies + w_copies + list(f_copies.values())
    outgoing += st_copies + c_copies
    for copy in outgoing:
        copy.wait_send()

    @pl.when(inner)
    def _():
        for i in (2, 3):
            pltpu.make_async_remote_copy(
                src_ref=wbuf.at[0, plane],
                dst_ref=wbuf.at[0, plane],
                send_sem=w_send.at[i],
                recv_sem=w_recv.at[0],
                device_id=mate,
                device_id_type=MESH,
            ).wait_send()


def fused(keys, values, queries, learn_rate, w_gate, w_up, w_out):
    tokens, width = keys.shape
    hidden = w_gate.shape[1]
    planes = lax.axis_size("seq") // 2
    hb, db = hidden // 4, width // planes
    part_rows = 3 * hb
    vmem = pltpu.VMEM
    dma = pltpu.SemaphoreType.DMA
    scratch = [
        vmem((4 * tokens, width), BF16),
        vmem((4 * tokens, width), BF16),
        vmem((2 * tokens, width), BF16),
        vmem((width, 2 * hb), BF16),
        vmem((hb, width), BF16),
        vmem((tokens, width), BF16),
        vmem((1, tokens), F32),
        vmem((2, db, hidden), BF16),
        vmem((part_rows, db), F32),
        vmem((part_rows, db), F32),
        vmem((2 * hb, width), F32),
        vmem((hb, width), F32),
        vmem((3, part_rows, db), BF16),
        vmem((4, part_rows, db), BF16),
        vmem((4, 8, db), F32),
        vmem((planes, 8, db), F32),
        vmem((2, planes, part_rows, db), BF16),
        vmem((4 * hb, width), BF16),
        vmem((2 * hb, width), BF16),
        vmem((tokens, width), BF16),
        vmem((tokens, width), BF16),
        dma((2, 3)),
        dma((2, 3)),
        dma,
        dma,
        dma((3,)),
        dma((4,)),
        dma((3,)),
        dma((3,)),
        dma((planes - 1,)),
        dma((planes,)),
        dma((4,)),
        dma((planes,)),
        dma((planes,)),
        dma((planes,)),
        dma,
        dma,
        dma((9,)),
    ]
    return pl.pallas_call(
        functools.partial(kernel, planes),
        out_shape=jax.ShapeDtypeStruct((tokens, width), BF16),
        in_specs=[pl.BlockSpec(memory_space=pltpu.HBM)] * 7,
        out_specs=pl.BlockSpec(memory_space=pltpu.VMEM),
        scratch_shapes=scratch,
        compiler_params=pltpu.CompilerParams(
            collective_id=0, has_side_effects=True, vmem_limit_bytes=60 * 2**20
        ),
        cost_estimate=pl.CostEstimate(
            flops=2 * tokens * width * hidden * 9, bytes_accessed=2 * 2**20, transcendentals=0
        ),
    )(learn_rate.reshape(1, tokens), keys, values, queries, w_gate, w_up, w_out)


def renorm(weight, grads):
    old = weight.astype(F32)
    update = old + grads
    factor = jnp.sqrt(jnp.mean(old * old, axis=1, keepdims=True) + epsilon) / jnp.sqrt(
        jnp.mean(update * update, axis=1, keepdims=True) + epsilon
    )
    return (update * factor).astype(BF16)


def plain(keys, values, queries, learn_rate, w_gate, w_up, w_out):
    hidden = w_gate.shape[1]
    axes = ("seq", "outer")
    shards = lax.axis_size(axes)
    rows_in, rows_out = w_gate.shape[0] // shards, w_out.shape[0] // shards
    position = lax.axis_index(axes)
    scaled = (learn_rate[:, None] * values.astype(F32)).astype(BF16)
    gate_pre = jnp.dot(keys, w_gate, preferred_element_type=F32)
    up_pre = jnp.dot(keys, w_up, preferred_element_type=F32)
    back = lax.dot_general(scaled, w_out, NT, preferred_element_type=F32)
    activation = (jax.nn.silu(gate_pre) * up_pre).astype(BF16)
    d_gate = (back * up_pre * silu_grad(gate_pre)).astype(BF16)
    d_up = (back * jax.nn.silu(gate_pre)).astype(BF16)
    both = jnp.concatenate([d_gate, d_up], axis=1)
    full_in = lax.dot_general(keys, both, TN, preferred_element_type=F32)
    full_out = lax.dot_general(activation, scaled, TN, preferred_element_type=F32)
    grad_in = lax.psum_scatter(full_in, axes, scatter_dimension=0, tiled=True)
    grad_out = lax.psum_scatter(full_out, axes, scatter_dimension=0, tiled=True)
    own_gate = lax.dynamic_slice_in_dim(w_gate, position * rows_in, rows_in, 0)
    own_up = lax.dynamic_slice_in_dim(w_up, position * rows_in, rows_in, 0)
    own_out = lax.dynamic_slice_in_dim(w_out, position * rows_out, rows_out, 0)
    news = (
        renorm(own_gate, grad_in[:, :hidden]),
        renorm(own_up, grad_in[:, hidden:]),
        renorm(own_out, grad_out),
    )
    gate, up, out = [lax.all_gather(new, axes, axis=0, tiled=True) for new in news]
    q_gate = jnp.dot(queries, gate, preferred_element_type=F32)
    q_up = jnp.dot(queries, up, preferred_element_type=F32)
    q_act = (jax.nn.silu(q_gate) * q_up).astype(BF16)
    return jnp.dot(q_act, out, preferred_element_type=F32).astype(BF16)


def local(keys, values, queries, learn_rate, w_gate, w_up, w_out):
    width, hidden = w_gate.shape
    tokens = keys.shape[0]
    seq, cores = lax.axis_size("seq"), lax.axis_size("outer")
    planes = seq // 2
    fits = (
        cores == 2
        and seq % 2 == 0
        and planes == 4
        and width % (128 * planes) == 0
        and hidden % (4 * 32 * planes) == 0
        and hidden // 4 == 128
        and tokens == 128
    )
    chosen = fused if fits else plain
    return chosen(keys, values, queries, learn_rate, w_gate, w_up, w_out)


def solution(mesh):
    placed = (
        P(("grp", "seq", "outer"), None),
        P(("grp", "seq", "outer"), None),
        P(("grp", "seq", "outer"), None),
        P(("grp", "seq", "outer")),
        P("grp", None),
        P("grp", None),
        P("grp", None),
    )
    return jax.shard_map(
        local,
        mesh=mesh,
        in_specs=placed,
        out_specs=P(("grp", "seq", "outer"), None),
        check_vma=False,
    )
```

```python
import functools

import jax
import jax.numpy as jnp
from jax import lax
from jax.experimental import pallas as pl
from jax.experimental.pallas import tpu as pltpu
from jax.sharding import PartitionSpec as P

epsilon = 1e-06
MESH = pl.DeviceIdType.MESH
F32 = jnp.float32
BF16 = jnp.bfloat16
NT = (((1,), (1,)), ((), ()))
TN = (((0,), (0,)), ((), ()))


def silu_grad(inputs):
    sigma = jax.nn.sigmoid(inputs)
    return sigma * (1.0 + inputs * (1.0 - sigma))


def kernel(
    planes,
    lr_ref,
    k_ref,
    v_ref,
    q_ref,
    wg_ref,
    wu_ref,
    wo_ref,
    o_ref,
    kbuf,
    sbuf,
    qbuf,
    wcat,
    wback,
    vbuf,
    lrbuf,
    wrows,
    old,
    update,
    acc_in,
    acc_out,
    gsend,
    grecv,
    stat,
    fact,
    wbuf,
    wq,
    wo,
    psend,
    precv,
    tok_send,
    tok_recv,
    q_send,
    q_recv,
    g_send,
    g_recv,
    st_send,
    st_recv,
    f_send,
    f_recv,
    w_send,
    w_recv,
    c_send,
    c_recv,
    p_send,
    p_recv,
    load,
):
    tokens, width = k_ref.shape
    hidden = wg_ref.shape[1]
    hb = hidden // 4
    db = width // planes
    rb = hb // planes
    spread = width // db
    seq = lax.axis_index("seq")
    core = lax.axis_index("outer")
    plane, side = seq // 2, seq % 2
    quarter = side * 2 + core
    cols = pl.ds(pl.multiple_of(quarter * hb, hb), hb)

    inner = jnp.logical_or(plane == 1, plane == 2)
    outer = jnp.logical_not(inner)
    low_half = plane < 2
    buddy = jnp.where(low_half, 1 - plane, 5 - plane)
    fin = jnp.where(low_half, 2, 1)
    far = jnp.where(low_half, 3, 0)

    mate = {"outer": 1 - core}
    across = {"seq": plane * 2 + 1 - side}
    diagonal = {"seq": plane * 2 + 1 - side, "outer": 1 - core}

    def plane_at(distance):
        return (plane + distance) % planes

    def same_spot(distance):
        return {"seq": plane_at(distance) * 2 + side}

    def rows(slot):
        return pl.ds(slot * tokens, tokens)

    my_cols = pl.ds(pl.multiple_of(plane * db, db), db)
    moves = (
        (lr_ref, lrbuf),
        (v_ref, vbuf),
        (k_ref, kbuf.at[rows(0)]),
        (wg_ref.at[:, cols], wcat.at[:, 0:hb]),
        (wu_ref.at[:, cols], wcat.at[:, hb : 2 * hb]),
        (wo_ref.at[cols], wback),
        (wg_ref.at[my_cols], wrows.at[0]),
        (wu_ref.at[my_cols], wrows.at[1]),
        (q_ref, qbuf.at[rows(0)]),
    )
    loads = [pltpu.make_async_copy(a, b, load.at[i]) for i, (a, b) in enumerate(moves)]
    for copy in loads:
        copy.start()

    barrier = pltpu.get_barrier_semaphore()
    peers = [mate, across, diagonal] + [same_spot(d) for d in range(1, planes)]
    for peer in peers:
        pl.semaphore_signal(barrier, inc=1, device_id=peer, device_id_type=MESH)

    loads[0].wait()
    loads[1].wait()
    lr_cols = jnp.transpose(jnp.broadcast_to(lrbuf[...], (tokens, tokens)))
    rate = lr_cols[:, 0:1]
    sbuf[rows(0), :] = (rate * vbuf[...].astype(F32)).astype(BF16)
    pl.semaphore_wait(barrier, len(peers))

    def send(src, dst, send_sem, recv_sem, peer):
        copy = pltpu.make_async_remote_copy(
            src_ref=src,
            dst_ref=dst,
            send_sem=send_sem,
            recv_sem=recv_sem,
            device_id=peer,
            device_id_type=MESH,
        )
        copy.start()
        return copy

    def arrived(buf, recv_sem, peer, send_sem):
        pltpu.make_async_remote_copy(
            src_ref=buf,
            dst_ref=buf,
            send_sem=send_sem,
            recv_sem=recv_sem,
            device_id=peer,
            device_id_type=MESH,
        ).wait_recv()

    def token_copy(src, buf, kind, dst_slot, peer):
        return send(
            src,
            buf.at[rows(dst_slot)],
            tok_send.at[kind, dst_slot - 1],
            tok_recv.at[kind, dst_slot - 1],
            peer,
        )

    k_across = token_copy(k_ref, kbuf, 0, 2, across)
    s_across = token_copy(sbuf.at[rows(0)], sbuf, 1, 2, across)
    k_mate = token_copy(k_ref, kbuf, 0, 1, mate)
    s_mate = token_copy(sbuf.at[rows(0)], sbuf, 1, 1, mate)
    for copy in loads[2:]:
        copy.wait()

    old_sums = []
    for i in range(2):
        old[i * hb : (i + 1) * hb, :] = jnp.transpose(wrows[i, :, cols].astype(F32))
        whole = wrows[i].astype(F32)
        squares = whole * whole
        folded = squares[:, 0:hb]
        for j in range(1, 4):
            folded = folded + squares[:, j * hb : (j + 1) * hb]
        old_sums.append(jnp.sum(jnp.transpose(folded), axis=0, keepdims=True))
    old_out = wback[pl.ds(pl.multiple_of(plane * rb, rb), rb), :].astype(F32)
    for j in range(spread):
        old[2 * hb + j * rb : 2 * hb + (j + 1) * rb, :] = old_out[:, j * db : (j + 1) * db]

    def pre(span):
        both = jnp.dot(kbuf[span, :], wcat[...], preferred_element_type=F32)
        gate_pre, up_pre = both[:, 0:hb], both[:, hb : 2 * hb]
        sigma = jax.nn.sigmoid(gate_pre)
        swish = gate_pre * sigma
        act = (swish * up_pre).astype(BF16)
        slope = up_pre * (sigma * (1.0 + gate_pre * (1.0 - sigma)))
        return act, swish, slope

    def grads(span, act, swish, slope):
        back = lax.dot_general(sbuf[span, :], wback[...], NT, preferred_element_type=F32)
        d_gate = (back * slope).astype(BF16)
        d_up = (back * swish).astype(BF16)
        both = jnp.concatenate([d_gate, d_up], axis=1)
        g_in = lax.dot_general(both, kbuf[span, :], TN, preferred_element_type=F32)
        g_out = lax.dot_general(act, sbuf[span, :], TN, preferred_element_type=F32)
        return g_in, g_out

    k_mate.wait_recv()
    s_mate.wait_recv()
    first = slice(0, 2 * tokens)
    g_in, g_out = grads(first, *pre(first))
    acc_in[...] = g_in
    acc_out[...] = g_out

    k_across.wait_recv()
    k_forward = token_copy(kbuf.at[rows(2)], kbuf, 0, 3, mate)
    ready = pre(rows(2))
    k_forward.wait_recv()
    last = pre(rows(3))
    s_across.wait_recv()
    s_forward = token_copy(sbuf.at[rows(2)], sbuf, 1, 3, mate)
    q_copy = send(q_ref, qbuf.at[rows(1)], q_send, q_recv, across)
    g_in, g_out = grads(rows(2), *ready)
    acc_in[...] += g_in
    acc_out[...] += g_out
    s_forward.wait_recv()
    g_in, g_out = grads(rows(3), *last)
    acc_in[...] += g_in
    acc_out[...] += g_out

    def part(p):
        return acc_in[:, pl.ds(pl.multiple_of(p * db, db), db)], acc_out[
            pl.ds(pl.multiple_of(p * rb, rb), rb), :
        ]

    def stacked(p):
        top, low = part(p)
        return jnp.concatenate(
            [top] + [low[:, j * db : (j + 1) * db] for j in range(spread)], axis=0
        )

    def g_copy(i, dst, slot):
        return send(
            gsend.at[i], grecv.at[slot], g_send.at[i], g_recv.at[slot], {"seq": dst * 2 + side}
        )

    def g_arrived(slot):
        arrived(grecv.at[slot], g_recv.at[slot], mate, g_send.at[0])

    gsend[0] = stacked(jnp.where(outer, far, fin)).astype(BF16)
    g_copies = [g_copy(0, jnp.where(outer, buddy, fin), jnp.where(outer, 3, 0))]
    gsend[1] = stacked(jnp.where(outer, fin, buddy)).astype(BF16)

    @pl.when(outer)
    def _():
        g_copies[0].wait_send()

    g_copies.append(g_copy(1, jnp.where(outer, fin, buddy), jnp.where(outer, 1, 0)))

    @pl.when(outer)
    def _():
        gsend[2] = stacked(buddy).astype(BF16)

    @pl.when(inner)
    def _():
        g_arrived(3)
        gsend[2] = (stacked(far) + grecv[3].astype(F32)).astype(BF16)

    g_copies.append(g_copy(2, jnp.where(outer, buddy, far), jnp.where(outer, 2, 1)))
    update[...] = old[...] + stacked(plane)
    g_arrived(0)
    update[...] += grecv[0].astype(F32)

    @pl.when(inner)
    def _():
        g_arrived(2)
        update[...] += grecv[2].astype(F32)

    g_arrived(1)
    update[...] += grecv[1].astype(F32)
    sum_top = update[0 : 2 * hb, :]
    sum_low = [update[2 * hb + j * rb : 2 * hb + (j + 1) * rb, :] for j in range(spread)]

    squares = sum_top * sum_top
    mine = [
        jnp.sum(squares[i * hb : (i + 1) * hb, :], axis=0, keepdims=True) for i in range(2)
    ]
    stat[0] = jnp.concatenate([jnp.broadcast_to(one, (4, db)) for one in mine], axis=0)
    st_copies = [
        send(stat.at[0], stat.at[i + 1], st_send.at[i], st_recv.at[i], peer)
        for i, peer in enumerate((mate, across, diagonal))
    ]

    new_sum = sum(jnp.sum(one * one, axis=1, keepdims=True) for one in sum_low)
    old_sum = jnp.sum(old_out * old_out, axis=1, keepdims=True)
    factor = jnp.sqrt(old_sum / width + epsilon) / jnp.sqrt(new_sum / width + epsilon)
    wbuf[0, plane, 0 : 2 * hb, :] = sum_top.astype(BF16)
    for j in range(spread):
        wbuf[0, plane, 2 * hb + j * rb : 2 * hb + (j + 1) * rb, :] = (
            sum_low[j] * factor
        ).astype(BF16)

    def w_copy(i, p, dst):
        return send(
            wbuf.at[0, p], wbuf.at[0, p], w_send.at[i], w_recv.at[p], {"seq": dst * 2 + side}
        )

    w_copies = [w_copy(0, plane, jnp.where(outer, fin, buddy))]

    def to_mate(index, p):
        return send(wbuf.at[0, p], wbuf.at[1, p], c_send.at[index], c_recv.at[index], mate)

    c_copies = [to_mate(0, plane)]

    for copy in st_copies:
        copy.wait_recv()
    w_copies.append(w_copy(1, plane, jnp.where(outer, buddy, far)))

    @pl.when(inner)
    def _():
        w_copy(2, plane, fin)

    total = stat[0] + stat[1] + stat[2] + stat[3]
    olds = jnp.concatenate([jnp.broadcast_to(one, (4, db)) for one in old_sums], axis=0)
    fact[plane] = jnp.sqrt(olds / hidden + epsilon) / jnp.sqrt(total / hidden + epsilon)
    f_copies = {}
    for d in range(1, planes):
        f_copies[d] = send(
            fact.at[plane], fact.at[plane], f_send.at[d - 1], f_recv.at[plane], same_spot(d)
        )

    def place(which, p):
        to = pl.ds(pl.multiple_of(p * db, db), db)
        for i in range(2):
            rows_of = slice(i * hb, (i + 1) * hb)
            scaled = wbuf[which, p, rows_of, :].astype(F32) * fact[p, 4 * i : 4 * i + 1, :]
            wq[which * 2 * hb + i * hb : which * 2 * hb + (i + 1) * hb, to] = scaled.astype(BF16)
        for j in range(spread):
            wo[pl.ds(pl.multiple_of(which * hb + p * rb, rb), rb), j * db : (j + 1) * db] = wbuf[
                which, p, 2 * hb + j * rb : 2 * hb + (j + 1) * rb, :
            ]

    place(0, plane)
    arrived(wbuf.at[1, plane], c_recv.at[0], mate, c_send.at[0])
    place(1, plane)
    order = (
        jnp.where(outer, buddy, far),
        jnp.where(outer, fin, buddy),
        jnp.where(outer, far, fin),
    )
    for i, p in enumerate(order):
        arrived(wbuf.at[0, p], w_recv.at[p], mate, w_send.at[0])
        c_copies.append(to_mate(i + 1, p))
        if i == 0:

            @pl.when(inner)
            def _():
                w_copy(3, far, buddy)

        arrived(fact.at[p], f_recv.at[p], mate, f_send.at[0])
        place(0, p)
    q_copy.wait_recv()
    for i, p in enumerate(order):
        arrived(wbuf.at[1, p], c_recv.at[i + 1], mate, c_send.at[0])
        place(1, p)

    def apply(span):
        pres = lax.dot_general(qbuf[span, :], wq[...], NT, preferred_element_type=F32)
        acts = []
        for which in range(2):
            gate = pres[:, which * 2 * hb : which * 2 * hb + hb]
            up = pres[:, which * 2 * hb + hb : (which + 1) * 2 * hb]
            acts.append((gate * jax.nn.sigmoid(gate) * up).astype(BF16))
        return jnp.dot(jnp.concatenate(acts, axis=1), wo[...], preferred_element_type=F32)

    psend[...] = apply(slice(tokens, 2 * tokens)).astype(BF16)
    p_copy = send(psend, precv, p_send, p_recv, across)
    own = apply(slice(0, tokens))
    p_copy.wait_recv()
    o_ref[...] = (own + precv[...].astype(F32)).astype(BF16)

    outgoing = [k_across, s_across, k_mate, s_mate, k_forward, s_forward, q_copy, p_copy]
    outgoing += g_copies[1:] + w_copies + list(f_copies.values())
    outgoing += st_copies + c_copies
    for copy in outgoing:
        copy.wait_send()

    @pl.when(inner)
    def _():
        g_copies[0].wait_send()
        for i in (2, 3):
            pltpu.make_async_remote_copy(
                src_ref=wbuf.at[0, plane],
                dst_ref=wbuf.at[0, plane],
                send_sem=w_send.at[i],
                recv_sem=w_recv.at[0],
                device_id=mate,
                device_id_type=MESH,
            ).wait_send()


def fused(keys, values, queries, learn_rate, w_gate, w_up, w_out):
    tokens, width = keys.shape
    hidden = w_gate.shape[1]
    planes = lax.axis_size("seq") // 2
    hb, db = hidden // 4, width // planes
    part_rows = 3 * hb
    vmem = pltpu.VMEM
    dma = pltpu.SemaphoreType.DMA
    scratch = [
        vmem((4 * tokens, width), BF16),
        vmem((4 * tokens, width), BF16),
        vmem((2 * tokens, width), BF16),
        vmem((width, 2 * hb), BF16),
        vmem((hb, width), BF16),
        vmem((tokens, width), BF16),
        vmem((1, tokens), F32),
        vmem((2, db, hidden), BF16),
        vmem((part_rows, db), F32),
        vmem((part_rows, db), F32),
        vmem((2 * hb, width), F32),
        vmem((hb, width), F32),
        vmem((3, part_rows, db), BF16),
        vmem((4, part_rows, db), BF16),
        vmem((4, 8, db), F32),
        vmem((planes, 8, db), F32),
        vmem((2, planes, part_rows, db), BF16),
        vmem((4 * hb, width), BF16),
        vmem((2 * hb, width), BF16),
        vmem((tokens, width), BF16),
        vmem((tokens, width), BF16),
        dma((2, 3)),
        dma((2, 3)),
        dma,
        dma,
        dma((3,)),
        dma((4,)),
        dma((3,)),
        dma((3,)),
        dma((planes - 1,)),
        dma((planes,)),
        dma((4,)),
        dma((planes,)),
        dma((planes,)),
        dma((planes,)),
        dma,
        dma,
        dma((9,)),
    ]
    return pl.pallas_call(
        functools.partial(kernel, planes),
        out_shape=jax.ShapeDtypeStruct((tokens, width), BF16),
        in_specs=[pl.BlockSpec(memory_space=pltpu.HBM)] * 7,
        out_specs=pl.BlockSpec(memory_space=pltpu.VMEM),
        scratch_shapes=scratch,
        compiler_params=pltpu.CompilerParams(
            collective_id=0, has_side_effects=True, vmem_limit_bytes=215 * 2**18
        ),
        cost_estimate=pl.CostEstimate(
            flops=2 * tokens * width * hidden * 9, bytes_accessed=2 * 2**20, transcendentals=0
        ),
    )(learn_rate.reshape(1, tokens), keys, values, queries, w_gate, w_up, w_out)


def renorm(weight, grads):
    old = weight.astype(F32)
    update = old + grads
    factor = jnp.sqrt(jnp.mean(old * old, axis=1, keepdims=True) + epsilon) / jnp.sqrt(
        jnp.mean(update * update, axis=1, keepdims=True) + epsilon
    )
    return (update * factor).astype(BF16)


def plain(keys, values, queries, learn_rate, w_gate, w_up, w_out):
    hidden = w_gate.shape[1]
    axes = ("seq", "outer")
    shards = lax.axis_size(axes)
    rows_in, rows_out = w_gate.shape[0] // shards, w_out.shape[0] // shards
    position = lax.axis_index(axes)
    scaled = (learn_rate[:, None] * values.astype(F32)).astype(BF16)
    gate_pre = jnp.dot(keys, w_gate, preferred_element_type=F32)
    up_pre = jnp.dot(keys, w_up, preferred_element_type=F32)
    back = lax.dot_general(scaled, w_out, NT, preferred_element_type=F32)
    activation = (jax.nn.silu(gate_pre) * up_pre).astype(BF16)
    d_gate = (back * up_pre * silu_grad(gate_pre)).astype(BF16)
    d_up = (back * jax.nn.silu(gate_pre)).astype(BF16)
    both = jnp.concatenate([d_gate, d_up], axis=1)
    full_in = lax.dot_general(keys, both, TN, preferred_element_type=F32)
    full_out = lax.dot_general(activation, scaled, TN, preferred_element_type=F32)
    grad_in = lax.psum_scatter(full_in, axes, scatter_dimension=0, tiled=True)
    grad_out = lax.psum_scatter(full_out, axes, scatter_dimension=0, tiled=True)
    own_gate = lax.dynamic_slice_in_dim(w_gate, position * rows_in, rows_in, 0)
    own_up = lax.dynamic_slice_in_dim(w_up, position * rows_in, rows_in, 0)
    own_out = lax.dynamic_slice_in_dim(w_out, position * rows_out, rows_out, 0)
    news = (
        renorm(own_gate, grad_in[:, :hidden]),
        renorm(own_up, grad_in[:, hidden:]),
        renorm(own_out, grad_out),
    )
    gate, up, out = [lax.all_gather(new, axes, axis=0, tiled=True) for new in news]
    q_gate = jnp.dot(queries, gate, preferred_element_type=F32)
    q_up = jnp.dot(queries, up, preferred_element_type=F32)
    q_act = (jax.nn.silu(q_gate) * q_up).astype(BF16)
    return jnp.dot(q_act, out, preferred_element_type=F32).astype(BF16)


def local(keys, values, queries, learn_rate, w_gate, w_up, w_out):
    width, hidden = w_gate.shape
    tokens = keys.shape[0]
    seq, cores = lax.axis_size("seq"), lax.axis_size("outer")
    planes = seq // 2
    fits = (
        cores == 2
        and seq % 2 == 0
        and planes == 4
        and width % (128 * planes) == 0
        and hidden % (4 * 32 * planes) == 0
        and hidden // 4 == 128
        and tokens == 128
    )
    chosen = fused if fits else plain
    return chosen(keys, values, queries, learn_rate, w_gate, w_up, w_out)


def solution(mesh):
    placed = (
        P(("grp", "seq", "outer"), None),
        P(("grp", "seq", "outer"), None),
        P(("grp", "seq", "outer"), None),
        P(("grp", "seq", "outer")),
        P("grp", None),
        P("grp", None),
        P("grp", None),
    )
    return jax.shard_map(
        local,
        mesh=mesh,
        in_specs=placed,
        out_specs=P(("grp", "seq", "outer"), None),
        check_vma=False,
    )
```

```python
import functools

import jax
import jax.numpy as jnp
from jax import lax
from jax.experimental import pallas as pl
from jax.experimental.pallas import tpu as pltpu
from jax.sharding import PartitionSpec as P

epsilon = 1e-06
MESH = pl.DeviceIdType.MESH
F32 = jnp.float32
BF16 = jnp.bfloat16
NT = (((1,), (1,)), ((), ()))
TN = (((0,), (0,)), ((), ()))


def silu_grad(inputs):
    sigma = jax.nn.sigmoid(inputs)
    return sigma * (1.0 + inputs * (1.0 - sigma))


def kernel(
    planes,
    lr_ref,
    k_ref,
    v_ref,
    q_ref,
    wg_ref,
    wu_ref,
    wo_ref,
    o_ref,
    kbuf,
    sbuf,
    qbuf,
    wcat,
    wback,
    vbuf,
    lrbuf,
    wrows,
    old,
    update,
    acc_in,
    acc_out,
    gsend,
    grecv,
    stat,
    fact,
    wbuf,
    wq,
    wo,
    psend,
    precv,
    tok_send,
    tok_recv,
    q_send,
    q_recv,
    g_send,
    g_recv,
    st_send,
    st_recv,
    f_send,
    f_recv,
    w_send,
    w_recv,
    c_send,
    c_recv,
    p_send,
    p_recv,
    load,
):
    tokens, width = k_ref.shape
    hidden = wg_ref.shape[1]
    hb = hidden // 4
    db = width // planes
    rb = hb // planes
    spread = width // db
    seq = lax.axis_index("seq")
    core = lax.axis_index("outer")
    plane, side = seq // 2, seq % 2
    quarter = side * 2 + core
    cols = pl.ds(pl.multiple_of(quarter * hb, hb), hb)

    inner = jnp.logical_or(plane == 1, plane == 2)
    outer = jnp.logical_not(inner)
    low_half = plane < 2
    buddy = jnp.where(low_half, 1 - plane, 5 - plane)
    fin = jnp.where(low_half, 2, 1)
    far = jnp.where(low_half, 3, 0)

    mate = {"outer": 1 - core}
    across = {"seq": plane * 2 + 1 - side}
    diagonal = {"seq": plane * 2 + 1 - side, "outer": 1 - core}

    def plane_at(distance):
        return (plane + distance) % planes

    def same_spot(distance):
        return {"seq": plane_at(distance) * 2 + side}

    def rows(slot):
        return pl.ds(slot * tokens, tokens)

    my_cols = pl.ds(pl.multiple_of(plane * db, db), db)
    moves = (
        (lr_ref, lrbuf),
        (v_ref, vbuf),
        (k_ref, kbuf.at[rows(0)]),
        (wg_ref.at[:, cols], wcat.at[:, 0:hb]),
        (wu_ref.at[:, cols], wcat.at[:, hb : 2 * hb]),
        (wo_ref.at[cols], wback),
        (wg_ref.at[my_cols], wrows.at[0]),
        (wu_ref.at[my_cols], wrows.at[1]),
        (q_ref, qbuf.at[rows(0)]),
    )
    loads = [pltpu.make_async_copy(a, b, load.at[i]) for i, (a, b) in enumerate(moves)]
    for copy in loads:
        copy.start()

    barrier = pltpu.get_barrier_semaphore()
    peers = [mate, across, diagonal] + [same_spot(d) for d in range(1, planes)]
    for peer in peers:
        pl.semaphore_signal(barrier, inc=1, device_id=peer, device_id_type=MESH)

    loads[0].wait()
    loads[1].wait()
    lr_cols = jnp.transpose(jnp.broadcast_to(lrbuf[...], (tokens, tokens)))
    rate = lr_cols[:, 0:1]
    sbuf[rows(0), :] = (rate * vbuf[...].astype(F32)).astype(BF16)
    pl.semaphore_wait(barrier, len(peers))

    def send(src, dst, send_sem, recv_sem, peer):
        copy = pltpu.make_async_remote_copy(
            src_ref=src,
            dst_ref=dst,
            send_sem=send_sem,
            recv_sem=recv_sem,
            device_id=peer,
            device_id_type=MESH,
        )
        copy.start()
        return copy

    def arrived(buf, recv_sem, peer, send_sem):
        pltpu.make_async_remote_copy(
            src_ref=buf,
            dst_ref=buf,
            send_sem=send_sem,
            recv_sem=recv_sem,
            device_id=peer,
            device_id_type=MESH,
        ).wait_recv()

    def token_copy(src, buf, kind, dst_slot, peer):
        return send(
            src,
            buf.at[rows(dst_slot)],
            tok_send.at[kind, dst_slot - 1],
            tok_recv.at[kind, dst_slot - 1],
            peer,
        )

    k_mate = token_copy(k_ref, kbuf, 0, 1, mate)
    s_mate = token_copy(sbuf.at[rows(0)], sbuf, 1, 1, mate)
    k_across = token_copy(k_ref, kbuf, 0, 2, across)
    s_across = token_copy(sbuf.at[rows(0)], sbuf, 1, 2, across)
    for copy in loads[2:]:
        copy.wait()

    old_sums = []
    for i in range(2):
        old[i * hb : (i + 1) * hb, :] = jnp.transpose(wrows[i, :, cols].astype(F32))
        whole = wrows[i].astype(F32)
        squares = whole * whole
        folded = squares[:, 0:hb]
        for j in range(1, 4):
            folded = folded + squares[:, j * hb : (j + 1) * hb]
        old_sums.append(jnp.sum(jnp.transpose(folded), axis=0, keepdims=True))
    old_out = wback[pl.ds(pl.multiple_of(plane * rb, rb), rb), :].astype(F32)
    for j in range(spread):
        old[2 * hb + j * rb : 2 * hb + (j + 1) * rb, :] = old_out[:, j * db : (j + 1) * db]

    def pre(span):
        both = jnp.dot(kbuf[span, :], wcat[...], preferred_element_type=F32)
        gate_pre, up_pre = both[:, 0:hb], both[:, hb : 2 * hb]
        sigma = jax.nn.sigmoid(gate_pre)
        swish = gate_pre * sigma
        act = (swish * up_pre).astype(BF16)
        slope = up_pre * (sigma * (1.0 + gate_pre * (1.0 - sigma)))
        return act, swish, slope

    def grads(span, act, swish, slope):
        back = lax.dot_general(sbuf[span, :], wback[...], NT, preferred_element_type=F32)
        d_gate = (back * slope).astype(BF16)
        d_up = (back * swish).astype(BF16)
        both = jnp.concatenate([d_gate, d_up], axis=1)
        g_in = lax.dot_general(both, kbuf[span, :], TN, preferred_element_type=F32)
        g_out = lax.dot_general(act, sbuf[span, :], TN, preferred_element_type=F32)
        return g_in, g_out

    k_mate.wait_recv()
    s_mate.wait_recv()
    first = slice(0, 2 * tokens)
    g_in, g_out = grads(first, *pre(first))
    acc_in[...] = g_in
    acc_out[...] = g_out

    k_across.wait_recv()
    k_forward = token_copy(kbuf.at[rows(2)], kbuf, 0, 3, mate)
    ready = pre(rows(2))
    k_forward.wait_recv()
    last = pre(rows(3))
    s_across.wait_recv()
    s_forward = token_copy(sbuf.at[rows(2)], sbuf, 1, 3, mate)
    g_in, g_out = grads(rows(2), *ready)
    acc_in[...] += g_in
    acc_out[...] += g_out
    s_forward.wait_recv()
    g_in, g_out = grads(rows(3), *last)
    acc_in[...] += g_in
    acc_out[...] += g_out

    def part(p):
        return acc_in[:, pl.ds(pl.multiple_of(p * db, db), db)], acc_out[
            pl.ds(pl.multiple_of(p * rb, rb), rb), :
        ]

    def stacked(p):
        top, low = part(p)
        return jnp.concatenate(
            [top] + [low[:, j * db : (j + 1) * db] for j in range(spread)], axis=0
        )

    def g_copy(i, dst, slot):
        return send(
            gsend.at[i], grecv.at[slot], g_send.at[i], g_recv.at[slot], {"seq": dst * 2 + side}
        )

    def g_arrived(slot):
        arrived(grecv.at[slot], g_recv.at[slot], mate, g_send.at[0])

    gsend[0] = stacked(jnp.where(outer, far, fin)).astype(BF16)
    g_copies = [g_copy(0, jnp.where(outer, buddy, fin), jnp.where(outer, 3, 0))]
    gsend[1] = stacked(jnp.where(outer, fin, buddy)).astype(BF16)

    @pl.when(outer)
    def _():
        g_copies[0].wait_send()

    g_copies.append(g_copy(1, jnp.where(outer, fin, buddy), jnp.where(outer, 1, 0)))

    @pl.when(outer)
    def _():
        gsend[2] = stacked(buddy).astype(BF16)

    @pl.when(inner)
    def _():
        g_arrived(3)
        gsend[2] = (stacked(far) + grecv[3].astype(F32)).astype(BF16)

    g_copies.append(g_copy(2, jnp.where(outer, buddy, far), jnp.where(outer, 2, 1)))
    q_copy = send(q_ref, qbuf.at[rows(1)], q_send, q_recv, across)
    update[...] = old[...] + stacked(plane)
    g_arrived(0)
    update[...] += grecv[0].astype(F32)

    @pl.when(inner)
    def _():
        g_arrived(2)
        update[...] += grecv[2].astype(F32)

    g_arrived(1)
    update[...] += grecv[1].astype(F32)
    sum_top = update[0 : 2 * hb, :]
    sum_low = [update[2 * hb + j * rb : 2 * hb + (j + 1) * rb, :] for j in range(spread)]

    squares = sum_top * sum_top
    mine = [
        jnp.sum(squares[i * hb : (i + 1) * hb, :], axis=0, keepdims=True) for i in range(2)
    ]
    stat[0] = jnp.concatenate([jnp.broadcast_to(one, (4, db)) for one in mine], axis=0)
    st_copies = [
        send(stat.at[0], stat.at[i + 1], st_send.at[i], st_recv.at[i], peer)
        for i, peer in enumerate((mate, across, diagonal))
    ]

    new_sum = sum(jnp.sum(one * one, axis=1, keepdims=True) for one in sum_low)
    old_sum = jnp.sum(old_out * old_out, axis=1, keepdims=True)
    factor = jnp.sqrt(old_sum / width + epsilon) / jnp.sqrt(new_sum / width + epsilon)
    wbuf[0, plane, 0 : 2 * hb, :] = sum_top.astype(BF16)
    for j in range(spread):
        wbuf[0, plane, 2 * hb + j * rb : 2 * hb + (j + 1) * rb, :] = (
            sum_low[j] * factor
        ).astype(BF16)

    def w_copy(i, p, dst):
        return send(
            wbuf.at[0, p], wbuf.at[0, p], w_send.at[i], w_recv.at[p], {"seq": dst * 2 + side}
        )

    def to_mate(index, p):
        return send(wbuf.at[0, p], wbuf.at[1, p], c_send.at[index], c_recv.at[index], mate)

    c_copies = [to_mate(0, plane)]
    w_copies = [w_copy(0, plane, jnp.where(outer, fin, buddy))]

    for copy in st_copies:
        copy.wait_recv()
    w_copies.append(w_copy(1, plane, jnp.where(outer, buddy, far)))

    @pl.when(inner)
    def _():
        w_copy(2, plane, fin)

    total = stat[0] + stat[1] + stat[2] + stat[3]
    olds = jnp.concatenate([jnp.broadcast_to(one, (4, db)) for one in old_sums], axis=0)
    fact[plane] = jnp.sqrt(olds / hidden + epsilon) / jnp.sqrt(total / hidden + epsilon)
    f_copies = {}
    for d in range(1, planes):
        f_copies[d] = send(
            fact.at[plane], fact.at[plane], f_send.at[d - 1], f_recv.at[plane], same_spot(d)
        )

    def place(which, p):
        to = pl.ds(pl.multiple_of(p * db, db), db)
        for i in range(2):
            rows_of = slice(i * hb, (i + 1) * hb)
            scaled = wbuf[which, p, rows_of, :].astype(F32) * fact[p, 4 * i : 4 * i + 1, :]
            wq[which * 2 * hb + i * hb : which * 2 * hb + (i + 1) * hb, to] = scaled.astype(BF16)
        for j in range(spread):
            wo[pl.ds(pl.multiple_of(which * hb + p * rb, rb), rb), j * db : (j + 1) * db] = wbuf[
                which, p, 2 * hb + j * rb : 2 * hb + (j + 1) * rb, :
            ]

    place(0, plane)
    arrived(wbuf.at[1, plane], c_recv.at[0], mate, c_send.at[0])
    place(1, plane)
    order = (
        jnp.where(outer, buddy, far),
        jnp.where(outer, fin, buddy),
        jnp.where(outer, far, fin),
    )
    for i, p in enumerate(order):
        arrived(wbuf.at[0, p], w_recv.at[p], mate, w_send.at[0])
        c_copies.append(to_mate(i + 1, p))
        if i == 0:

            @pl.when(inner)
            def _():
                w_copy(3, far, buddy)

        arrived(fact.at[p], f_recv.at[p], mate, f_send.at[0])
        place(0, p)
    q_copy.wait_recv()
    for i, p in enumerate(order):
        arrived(wbuf.at[1, p], c_recv.at[i + 1], mate, c_send.at[0])
        place(1, p)

    def apply(span):
        pres = lax.dot_general(qbuf[span, :], wq[...], NT, preferred_element_type=F32)
        acts = []
        for which in range(2):
            gate = pres[:, which * 2 * hb : which * 2 * hb + hb]
            up = pres[:, which * 2 * hb + hb : (which + 1) * 2 * hb]
            acts.append((gate * jax.nn.sigmoid(gate) * up).astype(BF16))
        return jnp.dot(jnp.concatenate(acts, axis=1), wo[...], preferred_element_type=F32)

    psend[...] = apply(slice(tokens, 2 * tokens)).astype(BF16)
    p_copy = send(psend, precv, p_send, p_recv, across)
    own = apply(slice(0, tokens))
    p_copy.wait_recv()
    o_ref[...] = (own + precv[...].astype(F32)).astype(BF16)

    outgoing = [k_across, s_across, k_mate, s_mate, k_forward, s_forward, q_copy, p_copy]
    outgoing += g_copies[1:] + w_copies + list(f_copies.values())
    outgoing += st_copies + c_copies
    for copy in outgoing:
        copy.wait_send()

    @pl.when(inner)
    def _():
        g_copies[0].wait_send()
        for i in (2, 3):
            pltpu.make_async_remote_copy(
                src_ref=wbuf.at[0, plane],
                dst_ref=wbuf.at[0, plane],
                send_sem=w_send.at[i],
                recv_sem=w_recv.at[0],
                device_id=mate,
                device_id_type=MESH,
            ).wait_send()


def fused(keys, values, queries, learn_rate, w_gate, w_up, w_out):
    tokens, width = keys.shape
    hidden = w_gate.shape[1]
    planes = lax.axis_size("seq") // 2
    hb, db = hidden // 4, width // planes
    part_rows = 3 * hb
    vmem = pltpu.VMEM
    dma = pltpu.SemaphoreType.DMA
    scratch = [
        vmem((4 * tokens, width), BF16),
        vmem((4 * tokens, width), BF16),
        vmem((2 * tokens, width), BF16),
        vmem((width, 2 * hb), BF16),
        vmem((hb, width), BF16),
        vmem((tokens, width), BF16),
        vmem((1, tokens), F32),
        vmem((2, db, hidden), BF16),
        vmem((part_rows, db), F32),
        vmem((part_rows, db), F32),
        vmem((2 * hb, width), F32),
        vmem((hb, width), F32),
        vmem((3, part_rows, db), BF16),
        vmem((4, part_rows, db), BF16),
        vmem((4, 8, db), F32),
        vmem((planes, 8, db), F32),
        vmem((2, planes, part_rows, db), BF16),
        vmem((4 * hb, width), BF16),
        vmem((2 * hb, width), BF16),
        vmem((tokens, width), BF16),
        vmem((tokens, width), BF16),
        dma((2, 3)),
        dma((2, 3)),
        dma,
        dma,
        dma((3,)),
        dma((4,)),
        dma((3,)),
        dma((3,)),
        dma((planes - 1,)),
        dma((planes,)),
        dma((4,)),
        dma((planes,)),
        dma((planes,)),
        dma((planes,)),
        dma,
        dma,
        dma((9,)),
    ]
    return pl.pallas_call(
        functools.partial(kernel, planes),
        out_shape=jax.ShapeDtypeStruct((tokens, width), BF16),
        in_specs=[pl.BlockSpec(memory_space=pltpu.HBM)] * 7,
        out_specs=pl.BlockSpec(memory_space=pltpu.VMEM),
        scratch_shapes=scratch,
        compiler_params=pltpu.CompilerParams(
            collective_id=0, has_side_effects=True, vmem_limit_bytes=215 * 2**18
        ),
        cost_estimate=pl.CostEstimate(
            flops=2 * tokens * width * hidden * 9, bytes_accessed=2 * 2**20, transcendentals=0
        ),
    )(learn_rate.reshape(1, tokens), keys, values, queries, w_gate, w_up, w_out)


def renorm(weight, grads):
    old = weight.astype(F32)
    update = old + grads
    factor = jnp.sqrt(jnp.mean(old * old, axis=1, keepdims=True) + epsilon) / jnp.sqrt(
        jnp.mean(update * update, axis=1, keepdims=True) + epsilon
    )
    return (update * factor).astype(BF16)


def plain(keys, values, queries, learn_rate, w_gate, w_up, w_out):
    hidden = w_gate.shape[1]
    axes = ("seq", "outer")
    shards = lax.axis_size(axes)
    rows_in, rows_out = w_gate.shape[0] // shards, w_out.shape[0] // shards
    position = lax.axis_index(axes)
    scaled = (learn_rate[:, None] * values.astype(F32)).astype(BF16)
    gate_pre = jnp.dot(keys, w_gate, preferred_element_type=F32)
    up_pre = jnp.dot(keys, w_up, preferred_element_type=F32)
    back = lax.dot_general(scaled, w_out, NT, preferred_element_type=F32)
    activation = (jax.nn.silu(gate_pre) * up_pre).astype(BF16)
    d_gate = (back * up_pre * silu_grad(gate_pre)).astype(BF16)
    d_up = (back * jax.nn.silu(gate_pre)).astype(BF16)
    both = jnp.concatenate([d_gate, d_up], axis=1)
    full_in = lax.dot_general(keys, both, TN, preferred_element_type=F32)
    full_out = lax.dot_general(activation, scaled, TN, preferred_element_type=F32)
    grad_in = lax.psum_scatter(full_in, axes, scatter_dimension=0, tiled=True)
    grad_out = lax.psum_scatter(full_out, axes, scatter_dimension=0, tiled=True)
    own_gate = lax.dynamic_slice_in_dim(w_gate, position * rows_in, rows_in, 0)
    own_up = lax.dynamic_slice_in_dim(w_up, position * rows_in, rows_in, 0)
    own_out = lax.dynamic_slice_in_dim(w_out, position * rows_out, rows_out, 0)
    news = (
        renorm(own_gate, grad_in[:, :hidden]),
        renorm(own_up, grad_in[:, hidden:]),
        renorm(own_out, grad_out),
    )
    gate, up, out = [lax.all_gather(new, axes, axis=0, tiled=True) for new in news]
    q_gate = jnp.dot(queries, gate, preferred_element_type=F32)
    q_up = jnp.dot(queries, up, preferred_element_type=F32)
    q_act = (jax.nn.silu(q_gate) * q_up).astype(BF16)
    return jnp.dot(q_act, out, preferred_element_type=F32).astype(BF16)


def local(keys, values, queries, learn_rate, w_gate, w_up, w_out):
    width, hidden = w_gate.shape
    tokens = keys.shape[0]
    seq, cores = lax.axis_size("seq"), lax.axis_size("outer")
    planes = seq // 2
    fits = (
        cores == 2
        and seq % 2 == 0
        and planes == 4
        and width % (128 * planes) == 0
        and hidden % (4 * 32 * planes) == 0
        and hidden // 4 == 128
        and tokens == 128
    )
    chosen = fused if fits else plain
    return chosen(keys, values, queries, learn_rate, w_gate, w_up, w_out)


def solution(mesh):
    placed = (
        P(("grp", "seq", "outer"), None),
        P(("grp", "seq", "outer"), None),
        P(("grp", "seq", "outer"), None),
        P(("grp", "seq", "outer")),
        P("grp", None),
        P("grp", None),
        P("grp", None),
    )
    return jax.shard_map(
        local,
        mesh=mesh,
        in_specs=placed,
        out_specs=P(("grp", "seq", "outer"), None),
        check_vma=False,
    )
```

```python
import functools

import jax
import jax.numpy as jnp
from jax import lax
from jax.experimental import pallas as pl
from jax.experimental.pallas import tpu as pltpu
from jax.sharding import PartitionSpec as P

epsilon = 1e-06
MESH = pl.DeviceIdType.MESH
F32 = jnp.float32
BF16 = jnp.bfloat16
NT = (((1,), (1,)), ((), ()))
TN = (((0,), (0,)), ((), ()))


def silu_grad(inputs):
    sigma = jax.nn.sigmoid(inputs)
    return sigma * (1.0 + inputs * (1.0 - sigma))


def kernel(
    planes,
    lr_ref,
    k_ref,
    v_ref,
    q_ref,
    wg_ref,
    wu_ref,
    wo_ref,
    o_ref,
    kbuf,
    sbuf,
    qbuf,
    wcat,
    wback,
    vbuf,
    lrbuf,
    wrows,
    old,
    update,
    acc_in,
    acc_out,
    gsend,
    grecv,
    stat,
    fact,
    wbuf,
    wq,
    wo,
    psend,
    precv,
    tok_send,
    tok_recv,
    q_send,
    q_recv,
    g_send,
    g_recv,
    st_send,
    st_recv,
    f_send,
    f_recv,
    w_send,
    w_recv,
    c_send,
    c_recv,
    p_send,
    p_recv,
    load,
):
    tokens, width = k_ref.shape
    hidden = wg_ref.shape[1]
    hb = hidden // 4
    db = width // planes
    rb = hb // planes
    spread = width // db
    seq = lax.axis_index("seq")
    core = lax.axis_index("outer")
    plane, side = seq // 2, seq % 2
    quarter = side * 2 + core
    cols = pl.ds(pl.multiple_of(quarter * hb, hb), hb)

    inner = jnp.logical_or(plane == 1, plane == 2)
    outer = jnp.logical_not(inner)
    low_half = plane < 2
    buddy = jnp.where(low_half, 1 - plane, 5 - plane)
    fin = jnp.where(low_half, 2, 1)
    far = jnp.where(low_half, 3, 0)

    mate = {"outer": 1 - core}
    across = {"seq": plane * 2 + 1 - side}
    diagonal = {"seq": plane * 2 + 1 - side, "outer": 1 - core}

    def plane_at(distance):
        return (plane + distance) % planes

    def same_spot(distance):
        return {"seq": plane_at(distance) * 2 + side}

    barrier = pltpu.get_barrier_semaphore()
    peers = [mate, across, diagonal] + [same_spot(d) for d in range(1, planes)]
    for peer in peers:
        pl.semaphore_signal(barrier, inc=1, device_id=peer, device_id_type=MESH)

    def rows(slot):
        return pl.ds(slot * tokens, tokens)

    my_cols = pl.ds(pl.multiple_of(plane * db, db), db)
    moves = (
        (lr_ref, lrbuf),
        (v_ref, vbuf),
        (k_ref, kbuf.at[rows(0)]),
        (wg_ref.at[:, cols], wcat.at[:, 0:hb]),
        (wu_ref.at[:, cols], wcat.at[:, hb : 2 * hb]),
        (wo_ref.at[cols], wback),
        (wg_ref.at[my_cols], wrows.at[0]),
        (wu_ref.at[my_cols], wrows.at[1]),
        (q_ref, qbuf.at[rows(0)]),
    )
    loads = [pltpu.make_async_copy(a, b, load.at[i]) for i, (a, b) in enumerate(moves)]
    for copy in loads:
        copy.start()

    loads[0].wait()
    loads[1].wait()
    lr_cols = jnp.transpose(jnp.broadcast_to(lrbuf[...], (tokens, tokens)))
    rate = lr_cols[:, 0:1]
    sbuf[rows(0), :] = (rate * vbuf[...].astype(F32)).astype(BF16)
    pl.semaphore_wait(barrier, len(peers))

    def send(src, dst, send_sem, recv_sem, peer):
        copy = pltpu.make_async_remote_copy(
            src_ref=src,
            dst_ref=dst,
            send_sem=send_sem,
            recv_sem=recv_sem,
            device_id=peer,
            device_id_type=MESH,
        )
        copy.start()
        return copy

    def arrived(buf, recv_sem, peer, send_sem):
        pltpu.make_async_remote_copy(
            src_ref=buf,
            dst_ref=buf,
            send_sem=send_sem,
            recv_sem=recv_sem,
            device_id=peer,
            device_id_type=MESH,
        ).wait_recv()

    def token_copy(src, buf, kind, dst_slot, peer):
        return send(
            src,
            buf.at[rows(dst_slot)],
            tok_send.at[kind, dst_slot - 1],
            tok_recv.at[kind, dst_slot - 1],
            peer,
        )

    k_mate = token_copy(k_ref, kbuf, 0, 1, mate)
    s_mate = token_copy(sbuf.at[rows(0)], sbuf, 1, 1, mate)
    k_across = token_copy(k_ref, kbuf, 0, 2, across)
    s_across = token_copy(sbuf.at[rows(0)], sbuf, 1, 2, across)
    for copy in loads[2:]:
        copy.wait()

    old_sums = []
    for i in range(2):
        old[i * hb : (i + 1) * hb, :] = jnp.transpose(wrows[i, :, cols].astype(F32))
        whole = wrows[i].astype(F32)
        squares = whole * whole
        folded = squares[:, 0:hb]
        for j in range(1, 4):
            folded = folded + squares[:, j * hb : (j + 1) * hb]
        old_sums.append(jnp.sum(jnp.transpose(folded), axis=0, keepdims=True))
    old_out = wback[pl.ds(pl.multiple_of(plane * rb, rb), rb), :].astype(F32)
    for j in range(spread):
        old[2 * hb + j * rb : 2 * hb + (j + 1) * rb, :] = old_out[:, j * db : (j + 1) * db]

    def pre(span):
        both = jnp.dot(kbuf[span, :], wcat[...], preferred_element_type=F32)
        gate_pre, up_pre = both[:, 0:hb], both[:, hb : 2 * hb]
        sigma = jax.nn.sigmoid(gate_pre)
        swish = gate_pre * sigma
        act = (swish * up_pre).astype(BF16)
        slope = up_pre * (sigma * (1.0 + gate_pre * (1.0 - sigma)))
        return act, swish, slope

    def grads(span, act, swish, slope):
        back = lax.dot_general(sbuf[span, :], wback[...], NT, preferred_element_type=F32)
        d_gate = (back * slope).astype(BF16)
        d_up = (back * swish).astype(BF16)
        both = jnp.concatenate([d_gate, d_up], axis=1)
        g_in = lax.dot_general(both, kbuf[span, :], TN, preferred_element_type=F32)
        g_out = lax.dot_general(act, sbuf[span, :], TN, preferred_element_type=F32)
        return g_in, g_out

    k_mate.wait_recv()
    s_mate.wait_recv()
    first = slice(0, 2 * tokens)
    g_in, g_out = grads(first, *pre(first))
    acc_in[...] = g_in
    acc_out[...] = g_out

    k_across.wait_recv()
    k_forward = token_copy(kbuf.at[rows(2)], kbuf, 0, 3, mate)
    ready = pre(rows(2))
    k_forward.wait_recv()
    last = pre(rows(3))
    s_across.wait_recv()
    s_forward = token_copy(sbuf.at[rows(2)], sbuf, 1, 3, mate)
    g_in, g_out = grads(rows(2), *ready)
    acc_in[...] += g_in
    acc_out[...] += g_out
    s_forward.wait_recv()
    g_in, g_out = grads(rows(3), *last)
    acc_in[...] += g_in
    acc_out[...] += g_out

    def part(p):
        return acc_in[:, pl.ds(pl.multiple_of(p * db, db), db)], acc_out[
            pl.ds(pl.multiple_of(p * rb, rb), rb), :
        ]

    def stacked(p):
        top, low = part(p)
        return jnp.concatenate(
            [top] + [low[:, j * db : (j + 1) * db] for j in range(spread)], axis=0
        )

    def g_copy(i, dst, slot):
        return send(
            gsend.at[i], grecv.at[slot], g_send.at[i], g_recv.at[slot], {"seq": dst * 2 + side}
        )

    def g_arrived(slot):
        arrived(grecv.at[slot], g_recv.at[slot], mate, g_send.at[0])

    gsend[0] = stacked(jnp.where(outer, far, fin)).astype(BF16)
    g_copies = [g_copy(0, jnp.where(outer, buddy, fin), jnp.where(outer, 3, 0))]
    gsend[1] = stacked(jnp.where(outer, fin, buddy)).astype(BF16)

    @pl.when(outer)
    def _():
        g_copies[0].wait_send()

    g_copies.append(g_copy(1, jnp.where(outer, fin, buddy), jnp.where(outer, 1, 0)))

    @pl.when(outer)
    def _():
        gsend[2] = stacked(buddy).astype(BF16)

    @pl.when(inner)
    def _():
        g_arrived(3)
        gsend[2] = (stacked(far) + grecv[3].astype(F32)).astype(BF16)

    g_copies.append(g_copy(2, jnp.where(outer, buddy, far), jnp.where(outer, 2, 1)))
    q_copy = send(q_ref, qbuf.at[rows(1)], q_send, q_recv, across)
    update[...] = old[...] + stacked(plane)
    g_arrived(0)
    update[...] += grecv[0].astype(F32)

    @pl.when(inner)
    def _():
        g_arrived(2)
        update[...] += grecv[2].astype(F32)

    g_arrived(1)
    update[...] += grecv[1].astype(F32)
    sum_top = update[0 : 2 * hb, :]
    sum_low = [update[2 * hb + j * rb : 2 * hb + (j + 1) * rb, :] for j in range(spread)]

    squares = sum_top * sum_top
    mine = [
        jnp.sum(squares[i * hb : (i + 1) * hb, :], axis=0, keepdims=True) for i in range(2)
    ]
    stat[0] = jnp.concatenate([jnp.broadcast_to(one, (4, db)) for one in mine], axis=0)
    st_copies = [
        send(stat.at[0], stat.at[i + 1], st_send.at[i], st_recv.at[i], peer)
        for i, peer in enumerate((mate, across, diagonal))
    ]

    new_sum = sum(jnp.sum(one * one, axis=1, keepdims=True) for one in sum_low)
    old_sum = jnp.sum(old_out * old_out, axis=1, keepdims=True)
    factor = jnp.sqrt(old_sum / width + epsilon) / jnp.sqrt(new_sum / width + epsilon)
    wbuf[0, plane, 0 : 2 * hb, :] = sum_top.astype(BF16)
    for j in range(spread):
        wbuf[0, plane, 2 * hb + j * rb : 2 * hb + (j + 1) * rb, :] = (
            sum_low[j] * factor
        ).astype(BF16)

    def w_copy(i, p, dst):
        return send(
            wbuf.at[0, p], wbuf.at[0, p], w_send.at[i], w_recv.at[p], {"seq": dst * 2 + side}
        )

    def to_mate(index, p):
        return send(wbuf.at[0, p], wbuf.at[1, p], c_send.at[index], c_recv.at[index], mate)

    c_copies = [to_mate(0, plane)]
    w_copies = [w_copy(0, plane, jnp.where(outer, fin, buddy))]
    w_copies.append(w_copy(1, plane, jnp.where(outer, buddy, far)))

    @pl.when(inner)
    def _():
        w_copy(2, plane, fin)


    for copy in st_copies:
        copy.wait_recv()
    total = stat[0] + stat[1] + stat[2] + stat[3]
    olds = jnp.concatenate([jnp.broadcast_to(one, (4, db)) for one in old_sums], axis=0)
    fact[plane] = jnp.sqrt(olds / hidden + epsilon) / jnp.sqrt(total / hidden + epsilon)
    f_copies = {}
    for d in range(1, planes):
        f_copies[d] = send(
            fact.at[plane], fact.at[plane], f_send.at[d - 1], f_recv.at[plane], same_spot(d)
        )

    def place(which, p):
        to = pl.ds(pl.multiple_of(p * db, db), db)
        for i in range(2):
            rows_of = slice(i * hb, (i + 1) * hb)
            scaled = wbuf[which, p, rows_of, :].astype(F32) * fact[p, 4 * i : 4 * i + 1, :]
            wq[which * 2 * hb + i * hb : which * 2 * hb + (i + 1) * hb, to] = scaled.astype(BF16)
        for j in range(spread):
            wo[pl.ds(pl.multiple_of(which * hb + p * rb, rb), rb), j * db : (j + 1) * db] = wbuf[
                which, p, 2 * hb + j * rb : 2 * hb + (j + 1) * rb, :
            ]

    place(0, plane)
    arrived(wbuf.at[1, plane], c_recv.at[0], mate, c_send.at[0])
    place(1, plane)
    order = (
        jnp.where(outer, buddy, far),
        jnp.where(outer, fin, buddy),
        jnp.where(outer, far, fin),
    )

    def scale_first(p):
        arrived(fact.at[p], f_recv.at[p], mate, f_send.at[0])
        place(0, p)

    for i, p in enumerate(order):
        arrived(wbuf.at[0, p], w_recv.at[p], mate, w_send.at[0])
        c_copies.append(to_mate(i + 1, p))
        if i == 0:

            @pl.when(inner)
            def _():
                w_copy(3, far, buddy)

        if i == 1:
            scale_first(order[0])
    scale_first(order[1])
    scale_first(order[2])
    q_copy.wait_recv()
    for i, p in enumerate(order):
        arrived(wbuf.at[1, p], c_recv.at[i + 1], mate, c_send.at[0])
        place(1, p)

    def apply(span):
        pres = lax.dot_general(qbuf[span, :], wq[...], NT, preferred_element_type=F32)
        acts = []
        for which in range(2):
            gate = pres[:, which * 2 * hb : which * 2 * hb + hb]
            up = pres[:, which * 2 * hb + hb : (which + 1) * 2 * hb]
            acts.append((gate * jax.nn.sigmoid(gate) * up).astype(BF16))
        return jnp.dot(jnp.concatenate(acts, axis=1), wo[...], preferred_element_type=F32)

    half = tokens // 2
    p_copies = []
    for i in range(2):
        these = slice(i * half, (i + 1) * half)
        psend[these, :] = apply(slice(tokens + i * half, tokens + (i + 1) * half)).astype(BF16)
        p_copies.append(
            send(psend.at[these], precv.at[these], p_send.at[i], p_recv.at[i], across)
        )
    own = apply(slice(0, tokens))
    for i in range(2):
        these = slice(i * half, (i + 1) * half)
        p_copies[i].wait_recv()
        o_ref[these, :] = (own[these, :] + precv[these, :].astype(F32)).astype(BF16)

    outgoing = [k_across, s_across, k_mate, s_mate, k_forward, s_forward, q_copy] + p_copies
    outgoing += g_copies[1:] + w_copies + list(f_copies.values())
    outgoing += st_copies + c_copies
    for copy in outgoing:
        copy.wait_send()

    @pl.when(inner)
    def _():
        g_copies[0].wait_send()
        for i in (2, 3):
            pltpu.make_async_remote_copy(
                src_ref=wbuf.at[0, plane],
                dst_ref=wbuf.at[0, plane],
                send_sem=w_send.at[i],
                recv_sem=w_recv.at[0],
                device_id=mate,
                device_id_type=MESH,
            ).wait_send()


def fused(keys, values, queries, learn_rate, w_gate, w_up, w_out):
    tokens, width = keys.shape
    hidden = w_gate.shape[1]
    planes = lax.axis_size("seq") // 2
    hb, db = hidden // 4, width // planes
    part_rows = 3 * hb
    vmem = pltpu.VMEM
    dma = pltpu.SemaphoreType.DMA
    scratch = [
        vmem((4 * tokens, width), BF16),
        vmem((4 * tokens, width), BF16),
        vmem((2 * tokens, width), BF16),
        vmem((width, 2 * hb), BF16),
        vmem((hb, width), BF16),
        vmem((tokens, width), BF16),
        vmem((1, tokens), F32),
        vmem((2, db, hidden), BF16),
        vmem((part_rows, db), F32),
        vmem((part_rows, db), F32),
        vmem((2 * hb, width), F32),
        vmem((hb, width), F32),
        vmem((3, part_rows, db), BF16),
        vmem((4, part_rows, db), BF16),
        vmem((4, 8, db), F32),
        vmem((planes, 8, db), F32),
        vmem((2, planes, part_rows, db), BF16),
        vmem((4 * hb, width), BF16),
        vmem((2 * hb, width), BF16),
        vmem((tokens, width), BF16),
        vmem((tokens, width), BF16),
        dma((2, 3)),
        dma((2, 3)),
        dma,
        dma,
        dma((3,)),
        dma((4,)),
        dma((3,)),
        dma((3,)),
        dma((planes - 1,)),
        dma((planes,)),
        dma((4,)),
        dma((planes,)),
        dma((planes,)),
        dma((planes,)),
        dma((2,)),
        dma((2,)),
        dma((9,)),
    ]
    return pl.pallas_call(
        functools.partial(kernel, planes),
        out_shape=jax.ShapeDtypeStruct((tokens, width), BF16),
        in_specs=[pl.BlockSpec(memory_space=pltpu.HBM)] * 7,
        out_specs=pl.BlockSpec(memory_space=pltpu.VMEM),
        scratch_shapes=scratch,
        compiler_params=pltpu.CompilerParams(
            collective_id=0, has_side_effects=True, vmem_limit_bytes=215 * 2**18
        ),
        cost_estimate=pl.CostEstimate(
            flops=2 * tokens * width * hidden * 9, bytes_accessed=2 * 2**20, transcendentals=0
        ),
    )(learn_rate.reshape(1, tokens), keys, values, queries, w_gate, w_up, w_out)


def renorm(weight, grads):
    old = weight.astype(F32)
    update = old + grads
    factor = jnp.sqrt(jnp.mean(old * old, axis=1, keepdims=True) + epsilon) / jnp.sqrt(
        jnp.mean(update * update, axis=1, keepdims=True) + epsilon
    )
    return (update * factor).astype(BF16)


def plain(keys, values, queries, learn_rate, w_gate, w_up, w_out):
    hidden = w_gate.shape[1]
    axes = ("seq", "outer")
    shards = lax.axis_size(axes)
    rows_in, rows_out = w_gate.shape[0] // shards, w_out.shape[0] // shards
    position = lax.axis_index(axes)
    scaled = (learn_rate[:, None] * values.astype(F32)).astype(BF16)
    gate_pre = jnp.dot(keys, w_gate, preferred_element_type=F32)
    up_pre = jnp.dot(keys, w_up, preferred_element_type=F32)
    back = lax.dot_general(scaled, w_out, NT, preferred_element_type=F32)
    activation = (jax.nn.silu(gate_pre) * up_pre).astype(BF16)
    d_gate = (back * up_pre * silu_grad(gate_pre)).astype(BF16)
    d_up = (back * jax.nn.silu(gate_pre)).astype(BF16)
    both = jnp.concatenate([d_gate, d_up], axis=1)
    full_in = lax.dot_general(keys, both, TN, preferred_element_type=F32)
    full_out = lax.dot_general(activation, scaled, TN, preferred_element_type=F32)
    grad_in = lax.psum_scatter(full_in, axes, scatter_dimension=0, tiled=True)
    grad_out = lax.psum_scatter(full_out, axes, scatter_dimension=0, tiled=True)
    own_gate = lax.dynamic_slice_in_dim(w_gate, position * rows_in, rows_in, 0)
    own_up = lax.dynamic_slice_in_dim(w_up, position * rows_in, rows_in, 0)
    own_out = lax.dynamic_slice_in_dim(w_out, position * rows_out, rows_out, 0)
    news = (
        renorm(own_gate, grad_in[:, :hidden]),
        renorm(own_up, grad_in[:, hidden:]),
        renorm(own_out, grad_out),
    )
    gate, up, out = [lax.all_gather(new, axes, axis=0, tiled=True) for new in news]
    q_gate = jnp.dot(queries, gate, preferred_element_type=F32)
    q_up = jnp.dot(queries, up, preferred_element_type=F32)
    q_act = (jax.nn.silu(q_gate) * q_up).astype(BF16)
    return jnp.dot(q_act, out, preferred_element_type=F32).astype(BF16)


def local(keys, values, queries, learn_rate, w_gate, w_up, w_out):
    width, hidden = w_gate.shape
    tokens = keys.shape[0]
    seq, cores = lax.axis_size("seq"), lax.axis_size("outer")
    planes = seq // 2
    fits = (
        cores == 2
        and seq % 2 == 0
        and planes == 4
        and width % (128 * planes) == 0
        and hidden % (4 * 32 * planes) == 0
        and hidden // 4 == 128
        and tokens == 128
    )
    chosen = fused if fits else plain
    return chosen(keys, values, queries, learn_rate, w_gate, w_up, w_out)


def solution(mesh):
    placed = (
        P(("grp", "seq", "outer"), None),
        P(("grp", "seq", "outer"), None),
        P(("grp", "seq", "outer"), None),
        P(("grp", "seq", "outer")),
        P("grp", None),
        P("grp", None),
        P("grp", None),
    )
    return jax.shard_map(
        local,
        mesh=mesh,
        in_specs=placed,
        out_specs=P(("grp", "seq", "outer"), None),
        check_vma=False,
    )
```

```python
import functools

import jax
import jax.numpy as jnp
from jax import lax
from jax.experimental import pallas as pl
from jax.experimental.pallas import tpu as pltpu
from jax.sharding import PartitionSpec as P

epsilon = 1e-06
MESH = pl.DeviceIdType.MESH
F32 = jnp.float32
BF16 = jnp.bfloat16
NT = (((1,), (1,)), ((), ()))
TN = (((0,), (0,)), ((), ()))


def silu_grad(inputs):
    sigma = jax.nn.sigmoid(inputs)
    return sigma * (1.0 + inputs * (1.0 - sigma))


def kernel(
    planes,
    lr_ref,
    k_ref,
    v_ref,
    q_ref,
    wg_ref,
    wu_ref,
    wo_ref,
    o_ref,
    kbuf,
    sbuf,
    qbuf,
    wcat,
    wback,
    vbuf,
    lrbuf,
    wrows,
    old,
    update,
    acc_in,
    acc_out,
    gsend,
    grecv,
    stat,
    fact,
    wbuf,
    wq,
    wo,
    psend,
    precv,
    tok_send,
    tok_recv,
    q_send,
    q_recv,
    g_send,
    g_recv,
    st_send,
    st_recv,
    f_send,
    f_recv,
    w_send,
    w_recv,
    c_send,
    c_recv,
    p_send,
    p_recv,
    load,
):
    tokens, width = k_ref.shape
    hidden = wg_ref.shape[1]
    hb = hidden // 4
    db = width // planes
    rb = hb // planes
    spread = width // db
    seq = lax.axis_index("seq")
    core = lax.axis_index("outer")
    plane, side = seq // 2, seq % 2
    quarter = side * 2 + core
    cols = pl.ds(pl.multiple_of(quarter * hb, hb), hb)

    inner = jnp.logical_or(plane == 1, plane == 2)
    outer = jnp.logical_not(inner)
    low_half = plane < 2
    buddy = jnp.where(low_half, 1 - plane, 5 - plane)
    fin = jnp.where(low_half, 2, 1)
    far = jnp.where(low_half, 3, 0)

    mate = {"outer": 1 - core}
    across = {"seq": plane * 2 + 1 - side}
    diagonal = {"seq": plane * 2 + 1 - side, "outer": 1 - core}

    def plane_at(distance):
        return (plane + distance) % planes

    def same_spot(distance):
        return {"seq": plane_at(distance) * 2 + side}

    barrier = pltpu.get_barrier_semaphore()
    peers = [mate, across, diagonal] + [same_spot(d) for d in range(1, planes)]
    for peer in peers:
        pl.semaphore_signal(barrier, inc=1, device_id=peer, device_id_type=MESH)

    def rows(slot):
        return pl.ds(slot * tokens, tokens)

    my_cols = pl.ds(pl.multiple_of(plane * db, db), db)
    moves = (
        (lr_ref, lrbuf),
        (v_ref, vbuf),
        (k_ref, kbuf.at[rows(0)]),
        (wg_ref.at[:, cols], wcat.at[:, 0:hb]),
        (wu_ref.at[:, cols], wcat.at[:, hb : 2 * hb]),
        (wo_ref.at[cols], wback),
        (wg_ref.at[my_cols], wrows.at[0]),
        (wu_ref.at[my_cols], wrows.at[1]),
        (q_ref, qbuf.at[rows(0)]),
    )
    loads = [pltpu.make_async_copy(a, b, load.at[i]) for i, (a, b) in enumerate(moves)]
    for copy in loads:
        copy.start()

    loads[0].wait()
    loads[1].wait()
    lr_cols = jnp.transpose(jnp.broadcast_to(lrbuf[...], (tokens, tokens)))
    rate = lr_cols[:, 0:1]
    sbuf[rows(0), :] = (rate * vbuf[...].astype(F32)).astype(BF16)
    pl.semaphore_wait(barrier, len(peers))

    def send(src, dst, send_sem, recv_sem, peer):
        copy = pltpu.make_async_remote_copy(
            src_ref=src,
            dst_ref=dst,
            send_sem=send_sem,
            recv_sem=recv_sem,
            device_id=peer,
            device_id_type=MESH,
        )
        copy.start()
        return copy

    def arrived(buf, recv_sem, peer, send_sem):
        pltpu.make_async_remote_copy(
            src_ref=buf,
            dst_ref=buf,
            send_sem=send_sem,
            recv_sem=recv_sem,
            device_id=peer,
            device_id_type=MESH,
        ).wait_recv()

    def token_copy(src, buf, kind, dst_slot, peer):
        return send(
            src,
            buf.at[rows(dst_slot)],
            tok_send.at[kind, dst_slot - 1],
            tok_recv.at[kind, dst_slot - 1],
            peer,
        )

    k_mate = token_copy(k_ref, kbuf, 0, 1, mate)
    s_mate = token_copy(sbuf.at[rows(0)], sbuf, 1, 1, mate)
    k_across = token_copy(k_ref, kbuf, 0, 2, across)
    s_across = token_copy(sbuf.at[rows(0)], sbuf, 1, 2, across)
    for copy in loads[2:]:
        copy.wait()

    old_sums = []
    for i in range(2):
        old[i * hb : (i + 1) * hb, :] = jnp.transpose(wrows[i, :, cols].astype(F32))
        whole = wrows[i].astype(F32)
        squares = whole * whole
        folded = squares[:, 0:hb]
        for j in range(1, 4):
            folded = folded + squares[:, j * hb : (j + 1) * hb]
        old_sums.append(jnp.sum(jnp.transpose(folded), axis=0, keepdims=True))
    old_out = wback[pl.ds(pl.multiple_of(plane * rb, rb), rb), :].astype(F32)
    for j in range(spread):
        old[2 * hb + j * rb : 2 * hb + (j + 1) * rb, :] = old_out[:, j * db : (j + 1) * db]

    def pre(span):
        both = jnp.dot(kbuf[span, :], wcat[...], preferred_element_type=F32)
        gate_pre, up_pre = both[:, 0:hb], both[:, hb : 2 * hb]
        sigma = jax.nn.sigmoid(gate_pre)
        swish = gate_pre * sigma
        act = (swish * up_pre).astype(BF16)
        slope = up_pre * (sigma * (1.0 + gate_pre * (1.0 - sigma)))
        return act, swish, slope

    def signals(span, swish, slope):
        back = lax.dot_general(sbuf[span, :], wback[...], NT, preferred_element_type=F32)
        d_gate = (back * slope).astype(BF16)
        d_up = (back * swish).astype(BF16)
        return jnp.concatenate([d_gate, d_up], axis=1)

    def grads(span, act, swish, slope):
        both = signals(span, swish, slope)
        g_in = lax.dot_general(both, kbuf[span, :], TN, preferred_element_type=F32)
        g_out = lax.dot_general(act, sbuf[span, :], TN, preferred_element_type=F32)
        return g_in, g_out

    k_mate.wait_recv()
    s_mate.wait_recv()
    first = slice(0, 2 * tokens)
    g_in, g_out = grads(first, *pre(first))
    acc_in[...] = g_in
    acc_out[...] = g_out

    k_across.wait_recv()
    k_forward = token_copy(kbuf.at[rows(2)], kbuf, 0, 3, mate)
    ready = pre(rows(2))
    k_forward.wait_recv()
    last = pre(rows(3))
    s_across.wait_recv()
    s_forward = token_copy(sbuf.at[rows(2)], sbuf, 1, 3, mate)
    g_in, g_out = grads(rows(2), *ready)
    acc_in[...] += g_in
    acc_out[...] += g_out
    s_forward.wait_recv()
    act, swish, slope = last
    both = signals(rows(3), swish, slope)
    acc_out[...] += lax.dot_general(act, sbuf[rows(3), :], TN, preferred_element_type=F32)
    lead = jnp.where(outer, far, fin)
    lead_cols = pl.ds(pl.multiple_of(lead * db, db), db)
    lead_in = lax.dot_general(both, kbuf[rows(3), lead_cols], TN, preferred_element_type=F32)

    def part(p):
        return acc_in[:, pl.ds(pl.multiple_of(p * db, db), db)], acc_out[
            pl.ds(pl.multiple_of(p * rb, rb), rb), :
        ]

    def stacked(p):
        top, low = part(p)
        return jnp.concatenate(
            [top] + [low[:, j * db : (j + 1) * db] for j in range(spread)], axis=0
        )

    def g_copy(i, dst, slot):
        return send(
            gsend.at[i], grecv.at[slot], g_send.at[i], g_recv.at[slot], {"seq": dst * 2 + side}
        )

    def g_arrived(slot):
        arrived(grecv.at[slot], g_recv.at[slot], mate, g_send.at[0])

    lead_top, lead_low = part(lead)
    gsend[0] = jnp.concatenate(
        [lead_top + lead_in] + [lead_low[:, j * db : (j + 1) * db] for j in range(spread)], axis=0
    ).astype(BF16)
    g_copies = [g_copy(0, jnp.where(outer, buddy, fin), jnp.where(outer, 3, 0))]
    acc_in[...] += lax.dot_general(both, kbuf[rows(3), :], TN, preferred_element_type=F32)
    gsend[1] = stacked(jnp.where(outer, fin, buddy)).astype(BF16)
    g_copies.append(g_copy(1, jnp.where(outer, fin, buddy), jnp.where(outer, 1, 0)))

    @pl.when(outer)
    def _():
        gsend[2] = stacked(buddy).astype(BF16)

    @pl.when(inner)
    def _():
        g_arrived(3)
        gsend[2] = (stacked(far) + grecv[3].astype(F32)).astype(BF16)

    g_copies.append(g_copy(2, jnp.where(outer, buddy, far), jnp.where(outer, 2, 1)))
    q_copy = send(q_ref, qbuf.at[rows(1)], q_send, q_recv, across)
    update[...] = old[...] + stacked(plane)
    g_arrived(0)
    update[...] += grecv[0].astype(F32)

    @pl.when(inner)
    def _():
        g_arrived(2)
        update[...] += grecv[2].astype(F32)

    g_arrived(1)
    update[...] += grecv[1].astype(F32)
    sum_top = update[0 : 2 * hb, :]
    sum_low = [update[2 * hb + j * rb : 2 * hb + (j + 1) * rb, :] for j in range(spread)]

    squares = sum_top * sum_top
    mine = [
        jnp.sum(squares[i * hb : (i + 1) * hb, :], axis=0, keepdims=True) for i in range(2)
    ]
    stat[0] = jnp.concatenate([jnp.broadcast_to(one, (4, db)) for one in mine], axis=0)
    st_copies = [
        send(stat.at[0], stat.at[i + 1], st_send.at[i], st_recv.at[i], peer)
        for i, peer in enumerate((mate, across, diagonal))
    ]

    new_sum = sum(jnp.sum(one * one, axis=1, keepdims=True) for one in sum_low)
    old_sum = jnp.sum(old_out * old_out, axis=1, keepdims=True)
    factor = jnp.sqrt(old_sum / width + epsilon) / jnp.sqrt(new_sum / width + epsilon)
    wbuf[0, plane, 0 : 2 * hb, :] = sum_top.astype(BF16)
    for j in range(spread):
        wbuf[0, plane, 2 * hb + j * rb : 2 * hb + (j + 1) * rb, :] = (
            sum_low[j] * factor
        ).astype(BF16)

    def w_copy(i, p, dst):
        return send(
            wbuf.at[0, p], wbuf.at[0, p], w_send.at[i], w_recv.at[p], {"seq": dst * 2 + side}
        )

    def to_mate(index, p):
        return send(wbuf.at[0, p], wbuf.at[1, p], c_send.at[index], c_recv.at[index], mate)

    c_copies = [to_mate(0, plane)]
    w_copies = [w_copy(0, plane, jnp.where(outer, fin, buddy))]
    w_copies.append(w_copy(1, plane, jnp.where(outer, buddy, far)))

    @pl.when(inner)
    def _():
        w_copy(2, plane, fin)


    for copy in st_copies:
        copy.wait_recv()
    total = stat[0] + stat[1] + stat[2] + stat[3]
    olds = jnp.concatenate([jnp.broadcast_to(one, (4, db)) for one in old_sums], axis=0)
    fact[plane] = jnp.sqrt(olds / hidden + epsilon) / jnp.sqrt(total / hidden + epsilon)
    f_copies = {}
    for d in range(1, planes):
        f_copies[d] = send(
            fact.at[plane], fact.at[plane], f_send.at[d - 1], f_recv.at[plane], same_spot(d)
        )

    def place(which, p):
        to = pl.ds(pl.multiple_of(p * db, db), db)
        for i in range(2):
            rows_of = slice(i * hb, (i + 1) * hb)
            scaled = wbuf[which, p, rows_of, :].astype(F32) * fact[p, 4 * i : 4 * i + 1, :]
            wq[which * 2 * hb + i * hb : which * 2 * hb + (i + 1) * hb, to] = scaled.astype(BF16)
        for j in range(spread):
            wo[pl.ds(pl.multiple_of(which * hb + p * rb, rb), rb), j * db : (j + 1) * db] = wbuf[
                which, p, 2 * hb + j * rb : 2 * hb + (j + 1) * rb, :
            ]

    place(0, plane)
    arrived(wbuf.at[1, plane], c_recv.at[0], mate, c_send.at[0])
    place(1, plane)
    order = (
        jnp.where(outer, buddy, far),
        jnp.where(outer, fin, buddy),
        jnp.where(outer, far, fin),
    )

    def scale_first(p):
        arrived(fact.at[p], f_recv.at[p], mate, f_send.at[0])
        place(0, p)

    for i, p in enumerate(order):
        arrived(wbuf.at[0, p], w_recv.at[p], mate, w_send.at[0])
        c_copies.append(to_mate(i + 1, p))
        if i == 0:

            @pl.when(inner)
            def _():
                w_copy(3, far, buddy)

        if i == 1:
            scale_first(order[0])
    scale_first(order[1])
    scale_first(order[2])
    q_copy.wait_recv()
    for i, p in enumerate(order):
        arrived(wbuf.at[1, p], c_recv.at[i + 1], mate, c_send.at[0])
        place(1, p)

    def apply(span):
        pres = lax.dot_general(qbuf[span, :], wq[...], NT, preferred_element_type=F32)
        acts = []
        for which in range(2):
            gate = pres[:, which * 2 * hb : which * 2 * hb + hb]
            up = pres[:, which * 2 * hb + hb : (which + 1) * 2 * hb]
            acts.append((gate * jax.nn.sigmoid(gate) * up).astype(BF16))
        return jnp.dot(jnp.concatenate(acts, axis=1), wo[...], preferred_element_type=F32)

    half = tokens // 2
    p_copies = []
    for i in range(2):
        these = slice(i * half, (i + 1) * half)
        psend[these, :] = apply(slice(tokens + i * half, tokens + (i + 1) * half)).astype(BF16)
        p_copies.append(
            send(psend.at[these], precv.at[these], p_send.at[i], p_recv.at[i], across)
        )
    own = apply(slice(0, tokens))
    for i in range(2):
        these = slice(i * half, (i + 1) * half)
        p_copies[i].wait_recv()
        o_ref[these, :] = (own[these, :] + precv[these, :].astype(F32)).astype(BF16)

    outgoing = [k_across, s_across, k_mate, s_mate, k_forward, s_forward, q_copy] + p_copies
    outgoing += g_copies + w_copies + list(f_copies.values())
    outgoing += st_copies + c_copies
    for copy in outgoing:
        copy.wait_send()

    @pl.when(inner)
    def _():
        for i in (2, 3):
            pltpu.make_async_remote_copy(
                src_ref=wbuf.at[0, plane],
                dst_ref=wbuf.at[0, plane],
                send_sem=w_send.at[i],
                recv_sem=w_recv.at[0],
                device_id=mate,
                device_id_type=MESH,
            ).wait_send()


def fused(keys, values, queries, learn_rate, w_gate, w_up, w_out):
    tokens, width = keys.shape
    hidden = w_gate.shape[1]
    planes = lax.axis_size("seq") // 2
    hb, db = hidden // 4, width // planes
    part_rows = 3 * hb
    vmem = pltpu.VMEM
    dma = pltpu.SemaphoreType.DMA
    scratch = [
        vmem((4 * tokens, width), BF16),
        vmem((4 * tokens, width), BF16),
        vmem((2 * tokens, width), BF16),
        vmem((width, 2 * hb), BF16),
        vmem((hb, width), BF16),
        vmem((tokens, width), BF16),
        vmem((1, tokens), F32),
        vmem((2, db, hidden), BF16),
        vmem((part_rows, db), F32),
        vmem((part_rows, db), F32),
        vmem((2 * hb, width), F32),
        vmem((hb, width), F32),
        vmem((3, part_rows, db), BF16),
        vmem((4, part_rows, db), BF16),
        vmem((4, 8, db), F32),
        vmem((planes, 8, db), F32),
        vmem((2, planes, part_rows, db), BF16),
        vmem((4 * hb, width), BF16),
        vmem((2 * hb, width), BF16),
        vmem((tokens, width), BF16),
        vmem((tokens, width), BF16),
        dma((2, 3)),
        dma((2, 3)),
        dma,
        dma,
        dma((3,)),
        dma((4,)),
        dma((3,)),
        dma((3,)),
        dma((planes - 1,)),
        dma((planes,)),
        dma((4,)),
        dma((planes,)),
        dma((planes,)),
        dma((planes,)),
        dma((2,)),
        dma((2,)),
        dma((9,)),
    ]
    return pl.pallas_call(
        functools.partial(kernel, planes),
        out_shape=jax.ShapeDtypeStruct((tokens, width), BF16),
        in_specs=[pl.BlockSpec(memory_space=pltpu.HBM)] * 7,
        out_specs=pl.BlockSpec(memory_space=pltpu.VMEM),
        scratch_shapes=scratch,
        compiler_params=pltpu.CompilerParams(
            collective_id=0, has_side_effects=True, vmem_limit_bytes=215 * 2**18
        ),
        cost_estimate=pl.CostEstimate(
            flops=2 * tokens * width * hidden * 9, bytes_accessed=2 * 2**20, transcendentals=0
        ),
    )(learn_rate.reshape(1, tokens), keys, values, queries, w_gate, w_up, w_out)


def renorm(weight, grads):
    old = weight.astype(F32)
    update = old + grads
    factor = jnp.sqrt(jnp.mean(old * old, axis=1, keepdims=True) + epsilon) / jnp.sqrt(
        jnp.mean(update * update, axis=1, keepdims=True) + epsilon
    )
    return (update * factor).astype(BF16)


def plain(keys, values, queries, learn_rate, w_gate, w_up, w_out):
    hidden = w_gate.shape[1]
    axes = ("seq", "outer")
    shards = lax.axis_size(axes)
    rows_in, rows_out = w_gate.shape[0] // shards, w_out.shape[0] // shards
    position = lax.axis_index(axes)
    scaled = (learn_rate[:, None] * values.astype(F32)).astype(BF16)
    gate_pre = jnp.dot(keys, w_gate, preferred_element_type=F32)
    up_pre = jnp.dot(keys, w_up, preferred_element_type=F32)
    back = lax.dot_general(scaled, w_out, NT, preferred_element_type=F32)
    activation = (jax.nn.silu(gate_pre) * up_pre).astype(BF16)
    d_gate = (back * up_pre * silu_grad(gate_pre)).astype(BF16)
    d_up = (back * jax.nn.silu(gate_pre)).astype(BF16)
    both = jnp.concatenate([d_gate, d_up], axis=1)
    full_in = lax.dot_general(keys, both, TN, preferred_element_type=F32)
    full_out = lax.dot_general(activation, scaled, TN, preferred_element_type=F32)
    grad_in = lax.psum_scatter(full_in, axes, scatter_dimension=0, tiled=True)
    grad_out = lax.psum_scatter(full_out, axes, scatter_dimension=0, tiled=True)
    own_gate = lax.dynamic_slice_in_dim(w_gate, position * rows_in, rows_in, 0)
    own_up = lax.dynamic_slice_in_dim(w_up, position * rows_in, rows_in, 0)
    own_out = lax.dynamic_slice_in_dim(w_out, position * rows_out, rows_out, 0)
    news = (
        renorm(own_gate, grad_in[:, :hidden]),
        renorm(own_up, grad_in[:, hidden:]),
        renorm(own_out, grad_out),
    )
    gate, up, out = [lax.all_gather(new, axes, axis=0, tiled=True) for new in news]
    q_gate = jnp.dot(queries, gate, preferred_element_type=F32)
    q_up = jnp.dot(queries, up, preferred_element_type=F32)
    q_act = (jax.nn.silu(q_gate) * q_up).astype(BF16)
    return jnp.dot(q_act, out, preferred_element_type=F32).astype(BF16)


def local(keys, values, queries, learn_rate, w_gate, w_up, w_out):
    width, hidden = w_gate.shape
    tokens = keys.shape[0]
    seq, cores = lax.axis_size("seq"), lax.axis_size("outer")
    planes = seq // 2
    fits = (
        cores == 2
        and seq % 2 == 0
        and planes == 4
        and width % (128 * planes) == 0
        and hidden % (4 * 32 * planes) == 0
        and hidden // 4 == 128
        and tokens == 128
    )
    chosen = fused if fits else plain
    return chosen(keys, values, queries, learn_rate, w_gate, w_up, w_out)


def solution(mesh):
    placed = (
        P(("grp", "seq", "outer"), None),
        P(("grp", "seq", "outer"), None),
        P(("grp", "seq", "outer"), None),
        P(("grp", "seq", "outer")),
        P("grp", None),
        P("grp", None),
        P("grp", None),
    )
    return jax.shard_map(
        local,
        mesh=mesh,
        in_specs=placed,
        out_specs=P(("grp", "seq", "outer"), None),
        check_vma=False,
    )
```
